32 devices in a mesh: expert: 8 (over y, x, core), dp: 4 (over z).
Axes of the slice: x: 2, y: 2, z: 4, core: 2. Of those that a mesh axis runs over, the one named last changes fastest.
Arguments:
- tokens: bfloat16 [4, 1024, 1536], P('dp', 'expert'), may hold values from -6 to 6
- out_cotangent: bfloat16 [4, 1024, 1536], P('dp', 'expert'), may hold values from -6 to 6
- chosen_rows: int32 [4, 8, 8, 16], P('dp', 'expert'), may hold values from 0 to 127, as said below
- counts: int32 [4, 8, 8], P('dp', 'expert'), may hold values from 0 to 16, as said below
- gate_weights: bfloat16 [4, 8, 8, 16], P('dp', 'expert'), may hold values from 0.099609375 to 1
- in_weights: bfloat16 [8, 1536, 1536], P('expert'), may hold values from -0.15625 to 0.15625
- down_weights: bfloat16 [8, 768, 1536], P('expert'), may hold values from -0.21875 to 0.21875
Outputs:
- token_grad: bfloat16 [4, 1024, 1536], P('dp', 'expert')
- gate_grad: bfloat16 [4, 8, 8, 16], P('dp', 'expert')
- in_grad: bfloat16 [8, 1536, 1536], P('expert', 'dp')
- down_grad: bfloat16 [8, 768, 1536], P('expert', None, 'dp')
The draws below stay inside these ranges and needn't reach their ends.
Inputs may be any that keep to these rules, and one draw needn't show every extreme that they name: `chosen_rows`: the entries of one device for one expert are distinct local token rows. For each expert and replica the counts over the 8 source devices sum to 64.
All inputs are finite; a program needn't handle non-finite values.
Results may differ from the reference program's by a relative error of at most 0.0095.
Values may be sent and summed in bfloat16 or wider, within the bound.
No kernel may reach another device: no remote copies, remote signals or barrier semaphores. Data moves between devices by JAX's collectives and lax.ppermute only.
A program may use at most 64 MiB of HBM per device.

```python
import jax
import jax.numpy as jnp
from jax import lax

D = 1536
H = 768
TOK_DEV = 128
SLOTS = 128
MOST = 16
EXPERTS = 8
N_EXPERT = 8
N_DP = 4


def draw_chosen_rows(key, part):
    key = jax.random.fold_in(key, 11)
    scores = jax.random.randint(key, (N_DP, N_EXPERT, EXPERTS, TOK_DEV), 0, 1 << 20, dtype=jnp.int32)
    scores = scores * TOK_DEV + jnp.arange(TOK_DEV, dtype=jnp.int32)
    shuffled = jnp.argsort(scores, axis=-1, stable=True)
    return shuffled[..., :MOST].astype(jnp.int32)


def draw_counts(key, part):
    key = jax.random.fold_in(key, 23)
    key_order, key_amount = jax.random.split(key)
    half_most = MOST // 2
    pair_count = N_EXPERT // 2
    scores = jax.random.randint(key_order, (N_DP, EXPERTS, N_EXPERT), 0, 1 << 20, dtype=jnp.int32)
    scores = scores * N_EXPERT + jnp.arange(N_EXPERT, dtype=jnp.int32)
    source_order = jnp.argsort(scores, axis=-1, stable=True).astype(jnp.int32)
    inverse = jnp.argsort(source_order, axis=-1, stable=True).astype(jnp.int32)
    amount = jax.random.randint(key_amount, (N_DP, EXPERTS, pair_count), 0, half_most + 1, dtype=jnp.int32)
    amount = amount.at[:, :, 0].set(half_most)
    deltas = jnp.stack([amount, -amount], axis=-1).reshape(N_DP, EXPERTS, N_EXPERT)
    placed = jnp.take_along_axis(deltas, inverse, axis=-1)
    result = half_most + placed
    return jnp.transpose(result, (0, 2, 1)).astype(jnp.int32)


def shard_levels(key, extent, shards, smallest, high):
    gain = 1.0
    for position, shards_of in shards:
        draws = jax.random.uniform(jax.random.fold_in(jax.random.fold_in(key, 6), position), (shards_of,), jnp.float32, smallest / len(shards), high / len(shards))
        gain = gain * jnp.repeat(jnp.exp(draws), extent[position] // shards_of).reshape((-1,) + (1,) * (len(extent) - 1 - position))
    return gain


def centred(key, extent, scale, most, cuts=(), held_as=jnp.bfloat16):
    values = scale * jax.random.normal(key, extent, jnp.float32)
    if cuts:
        values = values * shard_levels(key, extent, cuts, -0.22, 0.18)
    return jnp.clip(values, -most, most).astype(held_as)


def setup_inputs(seed: int = 0) -> dict:
    key_of = jax.random.split(jax.random.key(seed), 8)
    return {
        "tokens": centred(key_of[0], (N_DP, TOK_DEV * N_EXPERT, D), 1.0, 6.0, ((0, 4), (1, 8))),
        "out_cotangent": centred(key_of[1], (N_DP, TOK_DEV * N_EXPERT, D), 1.0, 6.0, ((0, 4), (1, 8))),
        "chosen_rows": draw_chosen_rows(jax.random.fold_in(key_of[7], 71), 0),
        "counts": draw_counts(jax.random.fold_in(key_of[7], 71), 0),
        "gate_weights": jnp.clip(0.099609375 + 0.9003906 * jax.random.uniform(key_of[4], (N_DP, N_EXPERT, EXPERTS, MOST), jnp.float32) ** shard_levels(key_of[4], (N_DP, N_EXPERT, EXPERTS, MOST), ((0, 4), (1, 8)), -0.2, 0.2), 0.099609375, 1.0).astype(jnp.bfloat16),
        "in_weights": centred(key_of[5], (EXPERTS, D, 2 * H), D ** -0.5, 0.15625, ((0, 8),)),
        "down_weights": centred(key_of[6], (EXPERTS, H, D), H ** -0.5, 0.21875, ((0, 8),)),
    }


def expert_pass(x_rows, cot_rows, gated, w_first, w_second):
    pre = jnp.dot(x_rows, w_first, preferred_element_type=jnp.float32)
    gate_pre = pre[:, :H]
    up_pre = pre[:, H:]
    squash = jax.nn.sigmoid(gate_pre)
    swished = gate_pre * squash
    hidden = (swished * up_pre).astype(jnp.bfloat16)
    slot_out = jnp.dot(hidden, w_second, preferred_element_type=jnp.float32)
    slot_gate = jnp.sum(slot_out * cot_rows.astype(jnp.float32), axis=-1).astype(jnp.bfloat16)
    scaled = (gated.astype(jnp.float32)[:, None] * cot_rows.astype(jnp.float32)).astype(jnp.bfloat16)
    hidden_grad = lax.dot_general(scaled, w_second, (((1,), (1,)), ((), ())), preferred_element_type=jnp.float32)
    pre_gate_grad = hidden_grad * up_pre * (squash * (1.0 + gate_pre * (1.0 - squash)))
    pre_up_grad = hidden_grad * swished
    in_rows = jnp.concatenate([pre_gate_grad, pre_up_grad], axis=1).astype(jnp.bfloat16)
    slot_grad = lax.dot_general(in_rows, w_first, (((1,), (1,)), ((), ())), preferred_element_type=jnp.float32).astype(jnp.bfloat16)
    in_term = lax.dot_general(x_rows, in_rows, (((0,), (0,)), ((), ())), preferred_element_type=jnp.float32).astype(jnp.bfloat16)
    down_term = lax.dot_general(hidden, scaled, (((0,), (0,)), ((), ())), preferred_element_type=jnp.float32).astype(jnp.bfloat16)
    return slot_grad, slot_gate, in_term, down_term


def reference(tokens, out_cotangent, chosen_rows, counts, gate_weights, in_weights, down_weights):
    slot_iota = jnp.arange(MOST, dtype=jnp.int32)
    offsets = (jnp.arange(N_EXPERT, dtype=jnp.int32) * TOK_DEV)[:, None, None]
    in_total = jnp.zeros((EXPERTS, D, 2 * H), jnp.float32)
    down_total = jnp.zeros((EXPERTS, H, D), jnp.float32)
    token_list = []
    gate_list = []
    for replica in range(N_DP):
        chosen = (chosen_rows[replica] + offsets).astype(jnp.int32)
        usable = slot_iota[None, None, :] < counts[replica][:, :, None]
        gated = jnp.where(usable, gate_weights[replica], jnp.zeros_like(gate_weights[replica]))
        row_index = jnp.transpose(chosen, (1, 0, 2)).reshape(EXPERTS, SLOTS)
        gate_slots = jnp.transpose(gated, (1, 0, 2)).reshape(EXPERTS, SLOTS)
        group_tokens = tokens[replica]
        group_cot = out_cotangent[replica]

        def per_expert(items):
            ident, gate_row, w_first, w_second = items
            return expert_pass(group_tokens[ident], group_cot[ident], gate_row, w_first, w_second)

        slot_grad, slot_gate, in_term, down_term = lax.map(per_expert, (row_index, gate_slots, in_weights, down_weights))
        in_total = in_total + in_term.astype(jnp.float32)
        down_total = down_total + down_term.astype(jnp.float32)
        summed = jnp.zeros((N_EXPERT * TOK_DEV, D), jnp.float32).at[row_index.reshape(-1)].add(slot_grad.reshape(-1, D).astype(jnp.float32))
        token_list.append(summed.astype(jnp.bfloat16))
        gate_back = jnp.transpose(slot_gate.reshape(EXPERTS, N_EXPERT, MOST), (1, 0, 2))
        gate_list.append(jnp.where(usable, gate_back, jnp.zeros_like(gate_back)))
    return jnp.stack(token_list), jnp.stack(gate_list), in_total.astype(jnp.bfloat16), down_total.astype(jnp.bfloat16)
```

```python
import functools

import jax
import jax.numpy as jnp
from jax import lax
from jax.experimental import pallas as pl
from jax.experimental.pallas import tpu as pltpu
from jax.sharding import PartitionSpec as P

F32 = jnp.float32
BF16 = jnp.bfloat16
USED = 64
LANES = 128

NEAR = ((0, 1), (1, 0), (2, 3), (3, 2))
MIDDLE = ((1, 2), (2, 1))
FAR = ((0, 2), (2, 0), (1, 3), (3, 1))
ONWARD = ((1, 0), (2, 3))


def dot_nn(left, right):
    return lax.dot_general(left, right, (((1,), (0,)), ((), ())), preferred_element_type=F32)


def dot_nt(left, right):
    return lax.dot_general(left, right, (((1,), (1,)), ((), ())), preferred_element_type=F32)


def dot_tn(left, right):
    return lax.dot_general(left, right, (((0,), (0,)), ((), ())), preferred_element_type=F32)


def iota(shape, dim):
    return lax.broadcasted_iota(jnp.int32, shape, dim)


def call(body, outs, args, flops, vmem=48):
    size = sum(a.size * a.dtype.itemsize for a in args) + sum(
        o.size * jnp.dtype(o.dtype).itemsize for o in outs
    )
    return pl.pallas_call(
        body,
        out_shape=tuple(outs),
        in_specs=[pl.BlockSpec(memory_space=pltpu.VMEM)] * len(args),
        out_specs=tuple(pl.BlockSpec(memory_space=pltpu.VMEM) for _ in outs),
        compiler_params=pltpu.CompilerParams(vmem_limit_bytes=vmem * 1024 * 1024),
        cost_estimate=pl.CostEstimate(flops=int(flops), bytes_accessed=int(size), transcendentals=0),
    )(*args)


def slot_maps(peers, most):
    slots = peers * most
    peer_hot = iota((slots, peers), 0) // most == iota((slots, peers), 1)
    k_hot = iota((slots, most), 0) % most == iota((slots, most), 1)
    return peer_hot, k_hot


def slot_column(values, peer_hot, k_hot):
    spread = dot_nn(peer_hot.astype(BF16), values)
    return jnp.sum(jnp.where(k_hot, spread, 0.0), axis=1, keepdims=True)


def token_hot(rows_ref, peer_hot, k_hot, tokens):
    column = slot_column(rows_ref[...].astype(F32).astype(BF16), peer_hot, k_hot)
    return iota((column.shape[0], tokens), 1) == column.astype(jnp.int32)


def used_column(counts_ref, peer_hot, most):
    slots = peer_hot.shape[0]
    count = jnp.sum(
        jnp.where(peer_hot, counts_ref[...].astype(F32), 0.0), axis=1, keepdims=True
    )
    return (iota((slots, 1), 0) % most).astype(F32) < count


def pick_tokens(rows_ref, counts_ref, tokens_ref, out_ref):
    peers, most = rows_ref.shape
    width = tokens_ref.shape[1]
    peer_hot, k_hot = slot_maps(peers, most)
    hot = token_hot(rows_ref, peer_hot, k_hot, tokens_ref.shape[0])
    used = used_column(counts_ref, peer_hot, most)
    out_ref[:, :width] = dot_nn(hot.astype(BF16), tokens_ref[...]).astype(BF16)
    out_ref[:, width:] = jnp.broadcast_to(
        jnp.where(used, 1.0, 0.0), (peers * most, LANES)
    ).astype(BF16)


def pick_scaled(rows_ref, counts_ref, gates_ref, cot_ref, out_ref):
    peers, most = rows_ref.shape
    peer_hot, k_hot = slot_maps(peers, most)
    hot = token_hot(rows_ref, peer_hot, k_hot, cot_ref.shape[0])
    used = used_column(counts_ref, peer_hot, most)
    gate = jnp.where(used, slot_column(gates_ref[...], peer_hot, k_hot), 0.0)
    out_ref[...] = (dot_nn(hot.astype(BF16), cot_ref[...]) * gate).astype(BF16)


def pack_tokens(arrived_ref, rows_ref, pack_ref):
    slots = arrived_ref.shape[0]
    width = rows_ref.shape[1]
    flags = arrived_ref[:, width:]
    before = (iota((slots, slots), 0) < iota((slots, slots), 1)).astype(BF16)
    same = (iota((slots, slots), 0) == iota((slots, slots), 1)).astype(BF16)
    place = dot_tn(flags, before)[:USED]
    used = dot_tn(flags, same)[:USED]
    row = iota((USED, slots), 0).astype(F32)
    pack = jnp.where(used > 0.5, jnp.where(place == row, 1.0, 0.0), 0.0).astype(BF16)
    pack_ref[...] = pack
    rows_ref[...] = dot_nn(pack, arrived_ref[:, :width]).astype(BF16)


def pack_scaled(arrived_ref, pack_ref, rows_ref):
    rows_ref[...] = dot_nn(pack_ref[...], arrived_ref[...]).astype(BF16)


def hidden_parts(x_rows, scaled, w_in, w_down):
    inner = w_down.shape[0]
    pre = dot_nn(x_rows, w_in)
    gate_pre = pre[:, :inner]
    up_pre = pre[:, inner:]
    squash = jax.nn.sigmoid(gate_pre)
    swished = gate_pre * squash
    hidden = (swished * up_pre).astype(BF16)
    hidden_grad = dot_nt(scaled, w_down)
    gate_grad = hidden_grad * up_pre * (squash * (1.0 + gate_pre * (1.0 - squash)))
    up_grad = hidden_grad * swished
    return hidden, hidden_grad, gate_grad.astype(BF16), up_grad.astype(BF16)


def own_rows(x_ref, scaled_ref, pack_ref, w_in_ref, w_down_ref, out_ref):
    inner = w_down_ref.shape[0]
    width = x_ref.shape[1]
    hidden, hidden_grad, gate_rows, up_rows = hidden_parts(
        x_ref[...], scaled_ref[...], w_in_ref[...], w_down_ref[...]
    )
    value = jnp.sum(hidden.astype(F32) * hidden_grad, axis=1, keepdims=True)
    high = value.astype(BF16).astype(F32)
    low = value - high
    lane = iota((x_ref.shape[0], LANES), 1)
    tail = jnp.where(lane == 0, high, jnp.where(lane == 1, low, 0.0)).astype(BF16)
    slot_grad = (
        dot_nt(gate_rows, w_in_ref[:, :inner]) + dot_nt(up_rows, w_in_ref[:, inner:])
    ).astype(BF16)
    pack = pack_ref[...]
    out_ref[:, :width] = dot_tn(pack, slot_grad).astype(BF16)
    out_ref[:, width:] = dot_tn(pack, tail).astype(BF16)


def combine_tokens(rows_ref, counts_ref, gates_ref, back_ref, token_ref, gate_ref):
    peers, most = rows_ref.shape
    tokens, width = token_ref.shape
    peer_hot, k_hot = slot_maps(peers, most)
    hot = token_hot(rows_ref, peer_hot, k_hot, tokens)
    used = used_column(counts_ref, peer_hot, most)
    token_ref[...] = dot_tn(hot.astype(BF16), back_ref[:, :width]).astype(BF16)
    tail = back_ref[:, width:].astype(F32)
    value = tail[:, 0:1] + tail[:, 1:2]
    gate = jnp.where(used, slot_column(gates_ref[...], peer_hot, k_hot), 1.0)
    value = jnp.where(used, value / gate, 0.0).astype(BF16).astype(F32)
    spread = jnp.where(k_hot, value, 0.0).astype(BF16)
    gate_ref[...] = dot_tn(peer_hot.astype(BF16), spread).astype(BF16)


def weight_grads(share, *refs):
    x_refs, s_refs = refs[:5], refs[5:10]
    index_ref, w_in_ref, w_down_ref, in_ref, down_ref, x_all, s_all = refs[10:]
    for held, blocks in ((x_all, x_refs), (s_all, s_refs)):
        for place in range(3):
            held[place * USED : (place + 1) * USED, :] = blocks[place][...]
        held[3 * USED :, :] = blocks[3][...] + blocks[4][...]
    inner = w_down_ref.shape[0]
    hidden, _, gate_rows, up_rows = hidden_parts(
        x_all[...], s_all[...], w_in_ref[...], w_down_ref[...]
    )
    start = pl.multiple_of(index_ref[0] * share, LANES)
    x_share = x_all[:, pl.ds(start, share)]
    s_share = s_all[:, pl.ds(start, share)]
    down_ref[...] = dot_tn(hidden, s_share).astype(BF16)
    in_ref[:, :inner] = dot_tn(x_share, gate_rows).astype(BF16)
    in_ref[:, inner:] = dot_tn(x_share, up_rows).astype(BF16)


def line_exchange(block):
    near = lax.ppermute(block, "dp", NEAR)
    far = lax.ppermute(block, "dp", FAR)
    middle = lax.ppermute(block, "dp", MIDDLE)
    onward = lax.ppermute(far, "dp", ONWARD)
    return block, near, far, middle, onward


def share_grads_on_line(x_rows, scaled, w_in, w_down, share):
    inner, width = w_down.shape
    x_blocks = line_exchange(x_rows)
    s_blocks = line_exchange(scaled)
    index = lax.axis_index("dp").astype(jnp.int32).reshape(1)
    args = (*x_blocks, *s_blocks, index, w_in, w_down)
    vmem = pl.BlockSpec(memory_space=pltpu.VMEM)
    rows = 4 * USED
    return pl.pallas_call(
        functools.partial(weight_grads, share),
        out_shape=(
            jax.ShapeDtypeStruct((share, 2 * inner), BF16),
            jax.ShapeDtypeStruct((inner, share), BF16),
        ),
        in_specs=[vmem] * 10 + [pl.BlockSpec(memory_space=pltpu.SMEM)] + [vmem] * 2,
        out_specs=(vmem, vmem),
        scratch_shapes=[pltpu.VMEM((rows, width), BF16)] * 2,
        compiler_params=pltpu.CompilerParams(vmem_limit_bytes=48 * 1024 * 1024),
        cost_estimate=pl.CostEstimate(
            flops=2 * rows * inner * (3 * width + 3 * share),
            bytes_accessed=2 * (3 * inner * width + 2 * rows * width + 3 * inner * share),
            transcendentals=rows * inner,
        ),
    )(*args)


def share_grads(x_rows, scaled, w_in, w_down, share):
    width = w_down.shape[1]
    x_all = lax.all_gather(x_rows, "dp", axis=0, tiled=True)
    s_all = lax.all_gather(scaled, "dp", axis=0, tiled=True)
    hidden, _, gate_rows, up_rows = hidden_parts(x_all, s_all, w_in, w_down)
    start = lax.axis_index("dp") * share
    x_share = lax.dynamic_slice_in_dim(x_all, start, share, axis=1)
    s_share = lax.dynamic_slice_in_dim(s_all, start, share, axis=1)
    in_grad = dot_tn(x_share, jnp.concatenate([gate_rows, up_rows], axis=1)).astype(BF16)
    return in_grad, dot_tn(hidden, s_share).astype(BF16)


def to_experts(block, peers):
    slots, width = block.shape
    moved = lax.all_to_all(
        block.reshape(peers, slots // peers, width), "expert", split_axis=0, concat_axis=0, tiled=True
    )
    return moved.reshape(slots, width)


def on_device(
    replicas, tokens, out_cotangent, chosen_rows, counts, gate_weights, in_weights, down_weights
):
    tokens, cot, w_in, w_down = tokens[0], out_cotangent[0], in_weights[0], down_weights[0]
    rows, count, gates = chosen_rows[0, 0], counts[0], gate_weights[0, 0]
    peers, most = rows.shape
    slots = peers * most
    n_tokens, width = tokens.shape
    inner = w_down.shape[0]
    shape = jax.ShapeDtypeStruct
    pick_flops = 2 * slots * n_tokens * width

    (x_sent,) = call(
        pick_tokens, [shape((slots, width + LANES), BF16)], (rows, count, tokens), pick_flops
    )
    x_arrived = to_experts(x_sent, peers)
    (s_sent,) = call(
        pick_scaled, [shape((slots, width), BF16)], (rows, count, gates, cot), pick_flops
    )
    s_arrived = to_experts(s_sent, peers)
    x_rows, pack = call(
        pack_tokens,
        [shape((USED, width), BF16), shape((USED, slots), BF16)],
        (x_arrived,),
        2 * USED * slots * width,
    )
    (scaled,) = call(
        pack_scaled, [shape((USED, width), BF16)], (s_arrived, pack), 2 * USED * slots * width
    )
    (sent_back,) = call(
        own_rows,
        [shape((slots, width + LANES), BF16)],
        (x_rows, scaled, pack, w_in, w_down),
        2 * USED * inner * width * 5,
    )
    back = to_experts(sent_back, peers)
    token_grad, gate_grad = call(
        combine_tokens,
        [shape((n_tokens, width), BF16), shape((peers, most), BF16)],
        (rows, count, gates, back),
        pick_flops,
    )
    share = width // replicas
    on_line = replicas == 4 and share % LANES == 0
    share_of = share_grads_on_line if on_line else share_grads
    in_grad, down_grad = share_of(x_rows, scaled, w_in, w_down, share)
    return (token_grad[None], gate_grad[None, None], in_grad[None], down_grad[None])


def solution(mesh):
    return jax.shard_map(
        functools.partial(on_device, mesh.shape["dp"]),
        mesh=mesh,
        in_specs=(
            P("dp", "expert", None),
            P("dp", "expert", None),
            P("dp", "expert", None, None),
            P("dp", "expert", None),
            P("dp", "expert", None, None),
            P("expert", None, None),
            P("expert", None, None),
        ),
        out_specs=(
            P("dp", "expert", None),
            P("dp", "expert", None, None),
            P("expert", "dp", None),
            P("expert", None, "dp"),
        ),
        check_vma=False,
    )
```

```python
import functools
import math

import jax
import jax.numpy as jnp
from jax import lax
from jax.experimental import pallas as pl
from jax.experimental.pallas import tpu as pltpu
from jax.sharding import PartitionSpec as P

F32 = jnp.float32
BF16 = jnp.bfloat16
USED = 64
LANES = 128

NEAR = ((0, 1), (1, 0), (2, 3), (3, 2))
MIDDLE = ((1, 2), (2, 1))
FAR = ((0, 2), (2, 0), (1, 3), (3, 1))
ONWARD = ((1, 0), (2, 3))
LOADS = ((0,), (1,), (2, 3), (3,))


def dot_nn(left, right):
    return lax.dot_general(left, right, (((1,), (0,)), ((), ())), preferred_element_type=F32)


def dot_nt(left, right):
    return lax.dot_general(left, right, (((1,), (1,)), ((), ())), preferred_element_type=F32)


def dot_tn(left, right):
    return lax.dot_general(left, right, (((0,), (0,)), ((), ())), preferred_element_type=F32)


def iota(shape, dim):
    return lax.broadcasted_iota(jnp.int32, shape, dim)


def call(body, outs, args, flops, in_specs=None, scratch=(), vmem=24, out_specs=None):
    size = sum(math.prod(a.shape) * a.dtype.itemsize for a in (*args, *outs))
    return pl.pallas_call(
        body,
        out_shape=tuple(outs),
        in_specs=in_specs or [pl.BlockSpec(memory_space=pltpu.VMEM)] * len(args),
        out_specs=tuple(out_specs or [pl.BlockSpec(memory_space=pltpu.VMEM) for _ in outs]),
        scratch_shapes=scratch,
        compiler_params=pltpu.CompilerParams(vmem_limit_bytes=vmem * 1024 * 1024),
        cost_estimate=pl.CostEstimate(flops=int(flops), bytes_accessed=int(size), transcendentals=0),
    )(*args)


def slot_maps(peers, most):
    slots = peers * most
    peer_hot = iota((slots, peers), 0) // most == iota((slots, peers), 1)
    k_hot = iota((slots, most), 0) % most == iota((slots, most), 1)
    return peer_hot, k_hot


def slot_column(values, peer_hot, k_hot):
    spread = dot_nn(peer_hot.astype(BF16), values)
    return jnp.sum(jnp.where(k_hot, spread, 0.0), axis=1, keepdims=True)


def token_hot(rows_ref, peer_hot, k_hot, tokens):
    column = slot_column(rows_ref[...].astype(F32).astype(BF16), peer_hot, k_hot)
    return iota((column.shape[0], tokens), 1) == column.astype(jnp.int32)


def used_column(counts, peer_hot, most):
    slots = peer_hot.shape[0]
    count = jnp.sum(jnp.where(peer_hot, counts.astype(F32), 0.0), axis=1, keepdims=True)
    return (iota((slots, 1), 0) % most).astype(F32) < count


def pick_rows(*refs):
    sources, out_ref, held, sems = refs[:5], refs[5], refs[6:11], refs[11]
    copies = [
        pltpu.make_async_copy(source, target, sems.at[place])
        for place, (source, target) in enumerate(zip(sources, held))
    ]
    for copy in copies:
        copy.start()
    rows_ref, counts_ref, gates_ref, tokens_ref, cot_ref = held
    peers, most = rows_ref.shape
    slots = peers * most
    width = tokens_ref.shape[1]
    peer_hot, k_hot = slot_maps(peers, most)
    for copy in copies[:3]:
        copy.wait()
    hot = token_hot(rows_ref, peer_hot, k_hot, tokens_ref.shape[0]).astype(BF16)
    used = used_column(counts_ref[...], peer_hot, most)
    gate = jnp.where(used, slot_column(gates_ref[...], peer_hot, k_hot), 0.0)
    out_ref[:, 2 * width :] = jnp.broadcast_to(jnp.where(used, 1.0, 0.0), (slots, LANES)).astype(BF16)
    copies[3].wait()
    out_ref[:, :width] = dot_nn(hot, tokens_ref[...]).astype(BF16)
    copies[4].wait()
    out_ref[:, width : 2 * width] = (dot_nn(hot, cot_ref[...]) * gate).astype(BF16)


def pack_matrix(flags):
    slots = flags.shape[0]
    before = (iota((slots, slots), 0) < iota((slots, slots), 1)).astype(BF16)
    same = (iota((slots, slots), 0) == iota((slots, slots), 1)).astype(BF16)
    place = dot_tn(flags, before)[:USED]
    used = dot_tn(flags, same)[:USED]
    row = iota((USED, slots), 0).astype(F32)
    return jnp.where(used > 0.5, jnp.where(place == row, 1.0, 0.0), 0.0).astype(BF16)


def pack_rows(arrived_ref, x_ref, pack_ref, x_keep_hbm, sem):
    width = x_ref.shape[1]
    pack = pack_matrix(arrived_ref[:, 2 * width :])
    pack_ref[...] = pack
    x_ref[...] = dot_nn(pack, arrived_ref[:, :width]).astype(BF16)
    keep = pltpu.make_async_copy(x_ref, x_keep_hbm, sem)
    keep.start()
    keep.wait()


def own_hidden_grad(share, index_ref, arrived_ref, pack_ref, w_down_ref, grad_ref, *refs):
    *load_refs, scaled_ref, own_ref, sem = refs
    inner, width = w_down_ref.shape
    scaled_ref[...] = dot_nn(pack_ref[...], arrived_ref[:, width : 2 * width]).astype(BF16)
    hidden_grad = dot_nt(scaled_ref[...], w_down_ref[...])
    grad_ref[...] = hidden_grad
    if not load_refs:
        return
    for load_ref, steps in zip((own_ref, *load_refs[1:]), LOADS):
        load_ref[:, :inner] = hidden_grad.astype(BF16)
        for place, step in enumerate(steps):
            start = pl.multiple_of((index_ref[0] ^ step) * share, LANES)
            load_ref[:, pl.ds(inner + place * share, share)] = scaled_ref[:, pl.ds(start, share)]
    keep = pltpu.make_async_copy(own_ref, load_refs[0], sem)
    keep.start()
    keep.wait()


def activations(pre, inner):
    gate_pre = pre[:, :inner]
    up_pre = pre[:, inner:]
    squash = jax.nn.sigmoid(gate_pre)
    swished = gate_pre * squash
    hidden = (swished * up_pre).astype(BF16)
    return hidden, up_pre * (squash * (1.0 + gate_pre * (1.0 - squash))), swished


def start_parts(source, target, sems, parts=4):
    depth = source.shape[0] // parts
    copies = []
    for part in range(parts):
        span = pl.ds(part * depth, depth)
        copies.append(pltpu.make_async_copy(source.at[span], target.at[span], sems.at[part]))
        copies[-1].start()
    return copies


def project(x, w_ref, copies):
    depth = w_ref.shape[0] // len(copies)
    total = None
    for part, copy in enumerate(copies):
        copy.wait()
        span = slice(part * depth, (part + 1) * depth)
        term = dot_nn(x[:, span], w_ref[span, :])
        total = term if total is None else total + term
    return total


def own_rows(x_ref, grad_ref, pack_ref, w_in_hbm, out_ref, w_in_ref, sems):
    inner = grad_ref.shape[1]
    width = w_in_ref.shape[0]
    copies = start_parts(w_in_hbm, w_in_ref, sems)
    hidden_grad = grad_ref[...]
    hidden, gate_factor, up_factor = activations(project(x_ref, w_in_ref, copies), inner)
    gate_rows = (hidden_grad * gate_factor).astype(BF16)
    up_rows = (hidden_grad * up_factor).astype(BF16)
    value = jnp.sum(hidden.astype(F32) * hidden_grad, axis=1, keepdims=True)
    high = value.astype(BF16).astype(F32)
    low = value - high
    lane = iota((x_ref.shape[0], LANES), 1)
    tail = jnp.where(lane == 0, high, jnp.where(lane == 1, low, 0.0)).astype(BF16)
    slot_grad = (
        dot_nt(gate_rows, w_in_ref[:, :inner]) + dot_nt(up_rows, w_in_ref[:, inner:])
    ).astype(BF16)
    pack = pack_ref[...]
    out_ref[:, :width] = dot_tn(pack, slot_grad).astype(BF16)
    out_ref[:, width:] = dot_tn(pack, tail).astype(BF16)


def combine_tokens(rows_ref, counts_ref, gates_ref, back_ref, token_ref, gate_ref):
    peers, most = rows_ref.shape
    tokens, width = token_ref.shape
    peer_hot, k_hot = slot_maps(peers, most)
    hot = token_hot(rows_ref, peer_hot, k_hot, tokens)
    used = used_column(counts_ref[...], peer_hot, most)
    token_ref[...] = dot_tn(hot.astype(BF16), back_ref[:, :width]).astype(BF16)
    value = back_ref[:, width : width + 1].astype(F32) + back_ref[:, width + 1 : width + 2].astype(F32)
    gate = jnp.where(used, slot_column(gates_ref[...], peer_hot, k_hot), 1.0)
    value = jnp.where(used, value / gate, 0.0).astype(BF16).astype(F32)
    spread = jnp.where(k_hot, value, 0.0).astype(BF16)
    gate_ref[...] = dot_tn(peer_hot.astype(BF16), spread).astype(BF16)


def near_rows(share, *refs):
    x_refs, load_refs, index_ref, w_in_ref = refs[:3], refs[3:6], refs[6], refs[7]
    w_in_held, x_share_ref, s_share_ref, hidden_ref, in_rows_ref, held, sems = refs[8:]
    copies = start_parts(w_in_ref, w_in_held, sems)
    inner = hidden_ref.shape[1]
    for place, ref in enumerate(x_refs):
        held[place * USED : (place + 1) * USED, :] = ref[...]
    x_share_ref[...] = held[:, pl.ds(pl.multiple_of(index_ref[0] * share, LANES), share)]
    hidden, gate_factor, up_factor = activations(project(held, w_in_held, copies), inner)
    hidden_ref[...] = hidden
    for place, ref in enumerate(load_refs):
        rows = slice(place * USED, (place + 1) * USED)
        grad = ref[:, :inner].astype(F32)
        in_rows_ref[rows, :inner] = (grad * gate_factor[rows]).astype(BF16)
        in_rows_ref[rows, inner:] = (grad * up_factor[rows]).astype(BF16)
        s_share_ref[rows, :] = ref[:, inner : inner + share]


def third_rows(
    share, middle_ref, onward_ref, index_ref, w_in_ref, x_share_ref, hidden_ref, gate_factor_ref, up_factor_ref, held
):
    held[...] = middle_ref[...] + onward_ref[...]
    x_share_ref[...] = held[:, pl.ds(pl.multiple_of(index_ref[0] * share, LANES), share)]
    hidden, gate_factor, up_factor = activations(dot_nn(held[...], w_in_ref[...]), hidden_ref.shape[1])
    hidden_ref[...] = hidden
    gate_factor_ref[...] = gate_factor
    up_factor_ref[...] = up_factor


def grads(middle_ref, onward_ref, *refs):
    first, third = refs[:4], refs[4:8]
    in_ref, down_ref, x_share, s_share, hidden, in_rows = refs[8:]
    inner, most, share = hidden.shape[1], 3 * USED, x_share.shape[1]
    for whole, part in zip((x_share, s_share, hidden, in_rows), first):
        whole[:most, :] = part[...]
    third_x_ref, third_hidden_ref, gate_factor_ref, up_factor_ref = third
    x_share[most:, :] = third_x_ref[...]
    hidden[most:, :] = third_hidden_ref[...]
    s_share[most:, :] = middle_ref[:, inner:] + onward_ref[:, inner + share :]
    grad = (middle_ref[:, :inner] + onward_ref[:, :inner]).astype(F32)
    in_rows[most:, :inner] = (grad * gate_factor_ref[...]).astype(BF16)
    in_rows[most:, inner:] = (grad * up_factor_ref[...]).astype(BF16)
    down_ref[...] = dot_tn(hidden[...], s_share[...]).astype(BF16)
    in_ref[...] = dot_tn(x_share[...], in_rows[...]).astype(BF16)


def to_experts(block, peers):
    slots, width = block.shape
    moved = lax.all_to_all(
        block.reshape(peers, slots // peers, width), "expert", split_axis=0, concat_axis=0, tiled=True
    )
    return moved.reshape(slots, width)


def on_device(
    replicas, tokens, out_cotangent, chosen_rows, counts, gate_weights, in_weights, down_weights
):
    tokens, cot, w_in, w_down = tokens[0], out_cotangent[0], in_weights[0], down_weights[0]
    rows, count, gates = chosen_rows[0, 0], counts[0], gate_weights[0, 0]
    peers, most = rows.shape
    slots = peers * most
    n_tokens, width = tokens.shape
    inner = w_down.shape[0]
    share = width // replicas
    on_line = replicas == 4 and share % LANES == 0
    index = lax.axis_index("dp").astype(jnp.int32).reshape(1)
    shape = jax.ShapeDtypeStruct
    vmem = pl.BlockSpec(memory_space=pltpu.VMEM)
    smem = pl.BlockSpec(memory_space=pltpu.SMEM)
    hbm = pl.BlockSpec(memory_space=pltpu.HBM)

    w_in_far = pltpu.with_memory_space_constraint(w_in, pltpu.HBM)
    picked = (rows, count, gates, tokens, cot)
    (sent,) = call(
        pick_rows,
        [shape((slots, 2 * width + LANES), BF16)],
        picked,
        4 * slots * n_tokens * width,
        [hbm] * 5,
        [pltpu.VMEM(a.shape, a.dtype) for a in picked] + [pltpu.SemaphoreType.DMA((5,))],
        56,
    )
    arrived = to_experts(sent, peers)
    x_rows, pack, x_keep = call(
        pack_rows,
        [shape((USED, width), BF16), shape((USED, slots), BF16), pltpu.HBM((USED, width), BF16)],
        (arrived,),
        2 * USED * slots * width,
        None,
        [pltpu.SemaphoreType.DMA],
        6,
        [vmem, vmem, hbm],
    )
    sizes = [inner + len(steps) * share for steps in LOADS]
    hidden_grad, *loads = call(
        functools.partial(own_hidden_grad, share),
        [shape((USED, inner), F32)]
        + [pltpu.HBM((USED, sizes[0]), BF16)] * on_line
        + [shape((USED, size), BF16) for size in sizes[1:]] * on_line,
        (index, arrived, pack, w_down),
        2 * USED * width * (slots + inner),
        [smem, vmem, vmem, vmem],
        [pltpu.VMEM((USED, width), BF16), pltpu.VMEM((USED, sizes[0]), BF16), pltpu.SemaphoreType.DMA],
        8,
        [vmem] + ([hbm] + [vmem] * 3) * on_line,
    )
    if on_line:
        own, near_load, far_load, middle_load = loads
        x_far = lax.ppermute(x_rows, "dp", FAR)
        x_near = lax.ppermute(x_rows, "dp", NEAR)
        far = lax.ppermute(far_load, "dp", FAR)
        near = lax.ppermute(near_load, "dp", NEAR)
        x_near, pack = lax.optimization_barrier((x_near, pack))
    parts = 4
    (sent_back,) = call(
        own_rows,
        [shape((slots, width + LANES), BF16)],
        (x_rows, hidden_grad, pack, w_in_far),
        2 * USED * inner * width * 4,
        [vmem] * 3 + [hbm],
        [pltpu.VMEM(w_in.shape, BF16), pltpu.SemaphoreType.DMA((parts,))],
        16,
    )
    back = to_experts(sent_back, peers)
    if on_line:
        x_far, sent_back = lax.optimization_barrier((x_far, sent_back))
        x_middle = lax.ppermute(x_rows, "dp", MIDDLE)
        middle = lax.ppermute(middle_load, "dp", MIDDLE)
        x_onward = lax.ppermute(x_far, "dp", ONWARD)
        onward = lax.ppermute(far, "dp", ONWARD)
    token_grad, gate_grad = call(
        combine_tokens,
        [shape((n_tokens, width), BF16), shape((peers, most), BF16)],
        (rows, count, gates, back),
        2 * slots * n_tokens * width,
        vmem=8,
    )
    if on_line:
        everyone, first = replicas * USED, 3 * USED

        w_in_held, *first_parts = call(
            functools.partial(near_rows, share),
            [
                shape(w_in.shape, BF16),
                shape((first, share), BF16),
                shape((first, share), BF16),
                shape((first, inner), BF16),
                shape((first, 2 * inner), BF16),
            ],
            (x_keep, x_near, x_far, own, near, far, index, w_in_far),
            4 * first * inner * width,
            [vmem] * 6 + [smem, hbm],
            [pltpu.VMEM((first, width), BF16), pltpu.SemaphoreType.DMA((parts,))],
            16,
        )
        third_parts = call(
            functools.partial(third_rows, share),
            [
                shape((USED, share), BF16),
                shape((USED, inner), BF16),
                shape((USED, inner), F32),
                shape((USED, inner), F32),
            ],
            (x_middle, x_onward, index, w_in_held),
            4 * USED * inner * width,
            [vmem] * 2 + [smem, vmem],
            [pltpu.VMEM((USED, width), BF16)],
            16,
        )
        middle, token_grad = lax.optimization_barrier((middle, token_grad))
        in_grad, down_grad = call(
            grads,
            [shape((share, 2 * inner), BF16), shape((inner, share), BF16)],
            (middle, onward, *first_parts, *third_parts),
            6 * everyone * inner * share,
            None,
            [
                pltpu.VMEM((everyone, share), BF16),
                pltpu.VMEM((everyone, share), BF16),
                pltpu.VMEM((everyone, inner), BF16),
                pltpu.VMEM((everyone, 2 * inner), BF16),
            ],
            16,
        )
    else:
        x_all = lax.all_gather(x_rows, "dp", axis=0, tiled=True)
        hidden, gate_factor, up_factor = activations(dot_nn(x_all, w_in), inner)
        hidden_grad = lax.all_gather(hidden_grad, "dp", axis=0, tiled=True)
        in_rows = jnp.concatenate([hidden_grad * gate_factor, hidden_grad * up_factor], axis=1)
        x_share = lax.dynamic_slice_in_dim(x_all, index[0] * share, share, axis=1)
        scaled = dot_nn(pack, arrived[:, width : 2 * width]).astype(BF16)
        s_all = lax.all_gather(scaled, "dp", axis=0, tiled=True)
        s_share = lax.dynamic_slice_in_dim(s_all, index[0] * share, share, axis=1)
        in_grad = dot_tn(x_share, in_rows.astype(BF16)).astype(BF16)
        down_grad = dot_tn(hidden, s_share).astype(BF16)
    return (token_grad[None], gate_grad[None, None], in_grad[None], down_grad[None])


def solution(mesh):
    return jax.shard_map(
        functools.partial(on_device, mesh.shape["dp"]),
        mesh=mesh,
        in_specs=(
            P("dp", "expert", None),
            P("dp", "expert", None),
            P("dp", "expert", None, None),
            P("dp", "expert", None),
            P("dp", "expert", None, None),
            P("expert", None, None),
            P("expert", None, None),
        ),
        out_specs=(
            P("dp", "expert", None),
            P("dp", "expert", None, None),
            P("expert", "dp", None),
            P("expert", None, "dp"),
        ),
        check_vma=False,
    )
```

```python
import functools
import math

import jax
import jax.numpy as jnp
from jax import lax
from jax.experimental import pallas as pl
from jax.experimental.pallas import tpu as pltpu
from jax.sharding import PartitionSpec as P

F32 = jnp.float32
BF16 = jnp.bfloat16
USED = 64
LANES = 128

NEAR = ((0, 1), (1, 0), (2, 3), (3, 2))
MIDDLE = ((1, 2), (2, 1))
FAR = ((0, 2), (2, 0), (1, 3), (3, 1))
ONWARD = ((1, 0), (2, 3))
LOADS = ((0,), (3,), (1,), (2, 3))


def dot_nn(left, right):
    return lax.dot_general(left, right, (((1,), (0,)), ((), ())), preferred_element_type=F32)


def dot_nt(left, right):
    return lax.dot_general(left, right, (((1,), (1,)), ((), ())), preferred_element_type=F32)


def dot_tn(left, right):
    return lax.dot_general(left, right, (((0,), (0,)), ((), ())), preferred_element_type=F32)


def iota(shape, dim):
    return lax.broadcasted_iota(jnp.int32, shape, dim)


def call(body, outs, args, flops, in_specs=None, scratch=(), vmem=24, out_specs=None):
    size = sum(math.prod(a.shape) * a.dtype.itemsize for a in (*args, *outs))
    return pl.pallas_call(
        body,
        out_shape=tuple(outs),
        in_specs=in_specs or [pl.BlockSpec(memory_space=pltpu.VMEM)] * len(args),
        out_specs=tuple(out_specs or [pl.BlockSpec(memory_space=pltpu.VMEM) for _ in outs]),
        scratch_shapes=scratch,
        compiler_params=pltpu.CompilerParams(vmem_limit_bytes=vmem * 1024 * 1024),
        cost_estimate=pl.CostEstimate(flops=int(flops), bytes_accessed=int(size), transcendentals=0),
    )(*args)


def slot_maps(peers, most):
    slots = peers * most
    peer_hot = iota((slots, peers), 0) // most == iota((slots, peers), 1)
    k_hot = iota((slots, most), 0) % most == iota((slots, most), 1)
    return peer_hot, k_hot


def slot_column(values, peer_hot, k_hot):
    spread = dot_nn(peer_hot.astype(BF16), values)
    return jnp.sum(jnp.where(k_hot, spread, 0.0), axis=1, keepdims=True)


def token_hot(rows_ref, peer_hot, k_hot, tokens):
    column = slot_column(rows_ref[...].astype(F32).astype(BF16), peer_hot, k_hot)
    return iota((column.shape[0], tokens), 1) == column.astype(jnp.int32)


def used_column(counts, peer_hot, most):
    slots = peer_hot.shape[0]
    count = jnp.sum(jnp.where(peer_hot, counts.astype(F32), 0.0), axis=1, keepdims=True)
    return (iota((slots, 1), 0) % most).astype(F32) < count


def pick_rows(*refs):
    sources, out_ref, held, sems = refs[:5], refs[5], refs[6:11], refs[11]
    copies = [
        pltpu.make_async_copy(source, target, sems.at[place])
        for place, (source, target) in enumerate(zip(sources, held))
    ]
    for copy in copies:
        copy.start()
    rows_ref, counts_ref, gates_ref, tokens_ref, cot_ref = held
    peers, most = rows_ref.shape
    slots = peers * most
    width = tokens_ref.shape[1]
    peer_hot, k_hot = slot_maps(peers, most)
    for copy in copies[:3]:
        copy.wait()
    hot = token_hot(rows_ref, peer_hot, k_hot, tokens_ref.shape[0]).astype(BF16)
    used = used_column(counts_ref[...], peer_hot, most)
    gate = jnp.where(used, slot_column(gates_ref[...], peer_hot, k_hot), 0.0)
    out_ref[:, 2 * width :] = jnp.broadcast_to(jnp.where(used, 1.0, 0.0), (slots, LANES)).astype(BF16)
    copies[3].wait()
    out_ref[:, :width] = dot_nn(hot, tokens_ref[...]).astype(BF16)
    copies[4].wait()
    out_ref[:, width : 2 * width] = (dot_nn(hot, cot_ref[...]) * gate).astype(BF16)


def pack_matrix(flags):
    slots = flags.shape[0]
    before = (iota((slots, slots), 0) < iota((slots, slots), 1)).astype(BF16)
    same = (iota((slots, slots), 0) == iota((slots, slots), 1)).astype(BF16)
    place = dot_tn(flags, before)[:USED]
    used = dot_tn(flags, same)[:USED]
    row = iota((USED, slots), 0).astype(F32)
    return jnp.where(used > 0.5, jnp.where(place == row, 1.0, 0.0), 0.0).astype(BF16)


def pack_rows(arrived_ref, x_ref, pack_ref):
    width = x_ref.shape[1]
    pack = pack_matrix(arrived_ref[:, 2 * width :])
    pack_ref[...] = pack
    x_ref[...] = dot_nn(pack, arrived_ref[:, :width]).astype(BF16)


def own_hidden_grad(share, index_ref, arrived_ref, pack_ref, x_ref, w_down_ref, grad_ref, *refs):
    *load_refs, scaled_ref, own_ref, middle_ref, sems = refs
    inner, width = w_down_ref.shape
    copies = []
    if load_refs:
        own_hbm, near_ref, far_ref, middle_hbm = load_refs
        for place, target in enumerate((own_hbm, middle_hbm)):
            x_part = target.at[:, pl.ds(inner + share, width)]
            copies.append(pltpu.make_async_copy(x_ref, x_part, sems.at[place]))
            copies[-1].start()
    scaled_ref[...] = dot_nn(pack_ref[...], arrived_ref[:, width : 2 * width]).astype(BF16)
    hidden_grad = dot_nt(scaled_ref[...], w_down_ref[...])
    grad_ref[...] = hidden_grad
    if not load_refs:
        return
    for place, (load_ref, steps) in enumerate(zip((own_ref, middle_ref, near_ref, far_ref), LOADS)):
        load_ref[:, :inner] = hidden_grad.astype(BF16)
        for part, step in enumerate(steps):
            start = pl.multiple_of((index_ref[0] ^ step) * share, LANES)
            load_ref[:, pl.ds(inner + part * share, share)] = scaled_ref[:, pl.ds(start, share)]
        if place < 2:
            load_part = (own_hbm, middle_hbm)[place].at[:, pl.ds(0, inner + share)]
            copies.append(pltpu.make_async_copy(load_ref, load_part, sems.at[2 + place]))
            copies[-1].start()
    for copy in copies:
        copy.wait()


def activations(pre, inner):
    gate_pre = pre[:, :inner]
    up_pre = pre[:, inner:]
    squash = jax.nn.sigmoid(gate_pre)
    swished = gate_pre * squash
    hidden = (swished * up_pre).astype(BF16)
    return hidden, up_pre * (squash * (1.0 + gate_pre * (1.0 - squash))), swished


def start_parts(source, target, sems, parts=4):
    depth = source.shape[0] // parts
    copies = []
    for part in range(parts):
        span = pl.ds(part * depth, depth)
        copies.append(pltpu.make_async_copy(source.at[span], target.at[span], sems.at[part]))
        copies[-1].start()
    return copies


def project(x, w_ref, copies):
    depth = w_ref.shape[0] // len(copies)
    total = None
    for part, copy in enumerate(copies):
        copy.wait()
        span = slice(part * depth, (part + 1) * depth)
        term = dot_nn(x[:, span], w_ref[span, :])
        total = term if total is None else total + term
    return total


def own_rows(x_ref, grad_ref, pack_ref, w_in_hbm, out_ref, w_in_ref, sems):
    inner = grad_ref.shape[1]
    width = w_in_ref.shape[0]
    copies = start_parts(w_in_hbm, w_in_ref, sems)
    hidden_grad = grad_ref[...]
    hidden, gate_factor, up_factor = activations(project(x_ref, w_in_ref, copies), inner)
    gate_rows = (hidden_grad * gate_factor).astype(BF16)
    up_rows = (hidden_grad * up_factor).astype(BF16)
    value = jnp.sum(hidden.astype(F32) * hidden_grad, axis=1, keepdims=True)
    high = value.astype(BF16).astype(F32)
    low = value - high
    lane = iota((x_ref.shape[0], LANES), 1)
    tail = jnp.where(lane == 0, high, jnp.where(lane == 1, low, 0.0)).astype(BF16)
    slot_grad = (
        dot_nt(gate_rows, w_in_ref[:, :inner]) + dot_nt(up_rows, w_in_ref[:, inner:])
    ).astype(BF16)
    pack = pack_ref[...]
    out_ref[:, :width] = dot_tn(pack, slot_grad).astype(BF16)
    out_ref[:, width:] = dot_tn(pack, tail).astype(BF16)


def combine_tokens(rows_ref, counts_ref, gates_ref, back_ref, token_ref, gate_ref):
    peers, most = rows_ref.shape
    tokens, width = token_ref.shape
    peer_hot, k_hot = slot_maps(peers, most)
    hot = token_hot(rows_ref, peer_hot, k_hot, tokens)
    used = used_column(counts_ref[...], peer_hot, most)
    token_ref[...] = dot_tn(hot.astype(BF16), back_ref[:, :width]).astype(BF16)
    value = back_ref[:, width : width + 1].astype(F32) + back_ref[:, width + 1 : width + 2].astype(F32)
    gate = jnp.where(used, slot_column(gates_ref[...], peer_hot, k_hot), 1.0)
    value = jnp.where(used, value / gate, 0.0).astype(BF16).astype(F32)
    spread = jnp.where(k_hot, value, 0.0).astype(BF16)
    gate_ref[...] = dot_tn(peer_hot.astype(BF16), spread).astype(BF16)


def near_rows(share, *refs):
    x_refs, load_refs, index_ref, w_in_ref = refs[:2], refs[2:5], refs[5], refs[6]
    w_in_held, x_share_ref, s_share_ref, hidden_ref, in_rows_ref, held, sems = refs[7:]
    copies = start_parts(w_in_ref, w_in_held, sems)
    inner = hidden_ref.shape[1]
    held[:USED, :] = load_refs[0][:, inner + share :]
    for place, ref in enumerate(x_refs, 1):
        held[place * USED : (place + 1) * USED, :] = ref[...]
    x_share_ref[...] = held[:, pl.ds(pl.multiple_of(index_ref[0] * share, LANES), share)]
    hidden, gate_factor, up_factor = activations(project(held, w_in_held, copies), inner)
    hidden_ref[...] = hidden
    for place, ref in enumerate(load_refs):
        rows = slice(place * USED, (place + 1) * USED)
        grad = ref[:, :inner].astype(F32)
        in_rows_ref[rows, :inner] = (grad * gate_factor[rows]).astype(BF16)
        in_rows_ref[rows, inner:] = (grad * up_factor[rows]).astype(BF16)
        s_share_ref[rows, :] = ref[:, inner : inner + share]


def third_rows(
    share, middle_ref, onward_ref, index_ref, w_in_ref, x_share_ref, hidden_ref, gate_factor_ref, up_factor_ref, held
):
    inner = hidden_ref.shape[1]
    held[...] = middle_ref[:, inner + share :] + onward_ref[...]
    x_share_ref[...] = held[:, pl.ds(pl.multiple_of(index_ref[0] * share, LANES), share)]
    hidden, gate_factor, up_factor = activations(dot_nn(held[...], w_in_ref[...]), hidden_ref.shape[1])
    hidden_ref[...] = hidden
    gate_factor_ref[...] = gate_factor
    up_factor_ref[...] = up_factor


def grads(middle_ref, onward_ref, *refs):
    first, third = refs[:4], refs[4:8]
    in_ref, down_ref, x_share, s_share, hidden, in_rows = refs[8:]
    inner, most, share = hidden.shape[1], 3 * USED, x_share.shape[1]
    for whole, part in zip((x_share, s_share, hidden, in_rows), first):
        whole[:most, :] = part[...]
    third_x_ref, third_hidden_ref, gate_factor_ref, up_factor_ref = third
    x_share[most:, :] = third_x_ref[...]
    hidden[most:, :] = third_hidden_ref[...]
    s_share[most:, :] = middle_ref[:, inner : inner + share] + onward_ref[:, inner + share :]
    grad = (middle_ref[:, :inner] + onward_ref[:, :inner]).astype(F32)
    in_rows[most:, :inner] = (grad * gate_factor_ref[...]).astype(BF16)
    in_rows[most:, inner:] = (grad * up_factor_ref[...]).astype(BF16)
    down_ref[...] = dot_tn(hidden[...], s_share[...]).astype(BF16)
    in_ref[...] = dot_tn(x_share[...], in_rows[...]).astype(BF16)


def to_experts(block, peers):
    slots, width = block.shape
    moved = lax.all_to_all(
        block.reshape(peers, slots // peers, width), "expert", split_axis=0, concat_axis=0, tiled=True
    )
    return moved.reshape(slots, width)


def on_device(
    replicas, tokens, out_cotangent, chosen_rows, counts, gate_weights, in_weights, down_weights
):
    tokens, cot, w_in, w_down = tokens[0], out_cotangent[0], in_weights[0], down_weights[0]
    rows, count, gates = chosen_rows[0, 0], counts[0], gate_weights[0, 0]
    peers, most = rows.shape
    slots = peers * most
    n_tokens, width = tokens.shape
    inner = w_down.shape[0]
    share = width // replicas
    on_line = replicas == 4 and share % LANES == 0
    index = lax.axis_index("dp").astype(jnp.int32).reshape(1)
    shape = jax.ShapeDtypeStruct
    vmem = pl.BlockSpec(memory_space=pltpu.VMEM)
    smem = pl.BlockSpec(memory_space=pltpu.SMEM)
    hbm = pl.BlockSpec(memory_space=pltpu.HBM)

    w_in_far = pltpu.with_memory_space_constraint(w_in, pltpu.HBM)
    picked = (rows, count, gates, tokens, cot)
    (sent,) = call(
        pick_rows,
        [shape((slots, 2 * width + LANES), BF16)],
        [pltpu.with_memory_space_constraint(a, pltpu.HBM) for a in picked],
        4 * slots * n_tokens * width,
        [hbm] * 5,
        [pltpu.VMEM(a.shape, a.dtype) for a in picked] + [pltpu.SemaphoreType.DMA((5,))],
        8,
    )
    arrived = to_experts(sent, peers)
    x_rows, pack = call(
        pack_rows,
        [shape((USED, width), BF16), shape((USED, slots), BF16)],
        (arrived,),
        2 * USED * slots * width,
        vmem=6,
    )
    short = inner + share
    hidden_grad, *loads = call(
        functools.partial(own_hidden_grad, share),
        [shape((USED, inner), F32)]
        + [
            pltpu.HBM((USED, short + width), BF16),
            shape((USED, short), BF16),
            shape((USED, short + share), BF16),
            pltpu.HBM((USED, short + width), BF16),
        ]
        * on_line,
        (index, arrived, pack, x_rows, w_down),
        2 * USED * width * (slots + inner),
        [smem] + [vmem] * 4,
        [
            pltpu.VMEM((USED, width), BF16),
            pltpu.VMEM((USED, short), BF16),
            pltpu.VMEM((USED, short), BF16),
            pltpu.SemaphoreType.DMA((4,)),
        ],
        8,
        [vmem] + [hbm, vmem, vmem, hbm] * on_line,
    )
    if on_line:
        own, near_load, far_load, middle_load = loads
        x_far = lax.ppermute(x_rows, "dp", FAR)
        x_near = lax.ppermute(x_rows, "dp", NEAR)
        far = lax.ppermute(far_load, "dp", FAR)
        near = lax.ppermute(near_load, "dp", NEAR)
    parts = 4
    (sent_back,) = call(
        own_rows,
        [shape((slots, width + LANES), BF16)],
        (x_rows, hidden_grad, pack, w_in_far),
        2 * USED * inner * width * 4,
        [vmem] * 3 + [hbm],
        [pltpu.VMEM(w_in.shape, BF16), pltpu.SemaphoreType.DMA((parts,))],
        16,
    )
    if on_line:
        x_near, near, sent_back = lax.optimization_barrier((x_near, near, sent_back))
    back = to_experts(sent_back, peers)
    if on_line:
        x_far, sent_back = lax.optimization_barrier((x_far, sent_back))
        middle = lax.ppermute(middle_load, "dp", MIDDLE)
        x_onward = lax.ppermute(x_far, "dp", ONWARD)
        onward = lax.ppermute(far, "dp", ONWARD)
    token_grad, gate_grad = call(
        combine_tokens,
        [shape((n_tokens, width), BF16), shape((peers, most), BF16)],
        (rows, count, gates, back),
        2 * slots * n_tokens * width,
        vmem=8,
    )
    if on_line:
        everyone, first = replicas * USED, 3 * USED

        w_in_held, *first_parts = call(
            functools.partial(near_rows, share),
            [
                shape(w_in.shape, BF16),
                shape((first, share), BF16),
                shape((first, share), BF16),
                shape((first, inner), BF16),
                shape((first, 2 * inner), BF16),
            ],
            (x_near, x_far, own, near, far, index, w_in_far),
            4 * first * inner * width,
            [vmem] * 5 + [smem, hbm],
            [pltpu.VMEM((first, width), BF16), pltpu.SemaphoreType.DMA((parts,))],
            16,
        )
        third_parts = call(
            functools.partial(third_rows, share),
            [
                shape((USED, share), BF16),
                shape((USED, inner), BF16),
                shape((USED, inner), F32),
                shape((USED, inner), F32),
            ],
            (middle, x_onward, index, w_in_held),
            4 * USED * inner * width,
            [vmem] * 2 + [smem, vmem],
            [pltpu.VMEM((USED, width), BF16)],
            16,
        )
        middle, token_grad = lax.optimization_barrier((middle, token_grad))
        in_grad, down_grad = call(
            grads,
            [shape((share, 2 * inner), BF16), shape((inner, share), BF16)],
            (middle, onward, *first_parts, *third_parts),
            6 * everyone * inner * share,
            None,
            [
                pltpu.VMEM((everyone, share), BF16),
                pltpu.VMEM((everyone, share), BF16),
                pltpu.VMEM((everyone, inner), BF16),
                pltpu.VMEM((everyone, 2 * inner), BF16),
            ],
            16,
        )
    else:
        x_all = lax.all_gather(x_rows, "dp", axis=0, tiled=True)
        hidden, gate_factor, up_factor = activations(dot_nn(x_all, w_in), inner)
        hidden_grad = lax.all_gather(hidden_grad, "dp", axis=0, tiled=True)
        in_rows = jnp.concatenate([hidden_grad * gate_factor, hidden_grad * up_factor], axis=1)
        x_share = lax.dynamic_slice_in_dim(x_all, index[0] * share, share, axis=1)
        scaled = dot_nn(pack, arrived[:, width : 2 * width]).astype(BF16)
        s_all = lax.all_gather(scaled, "dp", axis=0, tiled=True)
        s_share = lax.dynamic_slice_in_dim(s_all, index[0] * share, share, axis=1)
        in_grad = dot_tn(x_share, in_rows.astype(BF16)).astype(BF16)
        down_grad = dot_tn(hidden, s_share).astype(BF16)
    return (token_grad[None], gate_grad[None, None], in_grad[None], down_grad[None])


def solution(mesh):
    return jax.shard_map(
        functools.partial(on_device, mesh.shape["dp"]),
        mesh=mesh,
        in_specs=(
            P("dp", "expert", None),
            P("dp", "expert", None),
            P("dp", "expert", None, None),
            P("dp", "expert", None),
            P("dp", "expert", None, None),
            P("expert", None, None),
            P("expert", None, None),
        ),
        out_specs=(
            P("dp", "expert", None),
            P("dp", "expert", None, None),
            P("expert", "dp", None),
            P("expert", None, "dp"),
        ),
        check_vma=False,
    )
```

```python
import functools
import math

import jax
import jax.numpy as jnp
from jax import lax
from jax.experimental import pallas as pl
from jax.experimental.pallas import tpu as pltpu
from jax.sharding import PartitionSpec as P

F32 = jnp.float32
BF16 = jnp.bfloat16
USED = 64
LANES = 128

NEAR = ((0, 1), (1, 0), (2, 3), (3, 2))
MIDDLE = ((1, 2), (2, 1))
FAR = ((0, 2), (2, 0), (1, 3), (3, 1))
ONWARD = ((1, 0), (2, 3))
LOADS = ((0,), (3,), (1,), (2, 3))


def dot_nn(left, right):
    return lax.dot_general(left, right, (((1,), (0,)), ((), ())), preferred_element_type=F32)


def dot_nt(left, right):
    return lax.dot_general(left, right, (((1,), (1,)), ((), ())), preferred_element_type=F32)


def dot_tn(left, right):
    return lax.dot_general(left, right, (((0,), (0,)), ((), ())), preferred_element_type=F32)


def iota(shape, dim):
    return lax.broadcasted_iota(jnp.int32, shape, dim)


def call(body, outs, args, flops, in_specs=None, scratch=(), vmem=24, out_specs=None):
    size = sum(math.prod(a.shape) * a.dtype.itemsize for a in (*args, *outs))
    return pl.pallas_call(
        body,
        out_shape=tuple(outs),
        in_specs=in_specs or [pl.BlockSpec(memory_space=pltpu.VMEM)] * len(args),
        out_specs=tuple(out_specs or [pl.BlockSpec(memory_space=pltpu.VMEM) for _ in outs]),
        scratch_shapes=scratch,
        compiler_params=pltpu.CompilerParams(vmem_limit_bytes=vmem * 1024 * 1024),
        cost_estimate=pl.CostEstimate(flops=int(flops), bytes_accessed=int(size), transcendentals=0),
    )(*args)


def slot_maps(peers, most):
    slots = peers * most
    peer_hot = iota((slots, peers), 0) // most == iota((slots, peers), 1)
    k_hot = iota((slots, most), 0) % most == iota((slots, most), 1)
    return peer_hot, k_hot


def slot_column(values, peer_hot, k_hot):
    spread = dot_nn(peer_hot.astype(BF16), values)
    return jnp.sum(jnp.where(k_hot, spread, 0.0), axis=1, keepdims=True)


def token_hot(rows_ref, peer_hot, k_hot, tokens):
    column = slot_column(rows_ref[...].astype(F32).astype(BF16), peer_hot, k_hot)
    return iota((column.shape[0], tokens), 1) == column.astype(jnp.int32)


def used_column(counts, peer_hot, most):
    slots = peer_hot.shape[0]
    count = jnp.sum(jnp.where(peer_hot, counts.astype(F32), 0.0), axis=1, keepdims=True)
    return (iota((slots, 1), 0) % most).astype(F32) < count


def pick_rows(*refs):
    sources, out_ref, held, sems = refs[:5], refs[5], refs[6:11], refs[11]
    copies = [
        pltpu.make_async_copy(source, target, sems.at[place])
        for place, (source, target) in enumerate(zip(sources, held))
    ]
    for copy in copies:
        copy.start()
    rows_ref, counts_ref, gates_ref, tokens_ref, cot_ref = held
    peers, most = rows_ref.shape
    slots = peers * most
    width = tokens_ref.shape[1]
    peer_hot, k_hot = slot_maps(peers, most)
    for copy in copies[:3]:
        copy.wait()
    hot = token_hot(rows_ref, peer_hot, k_hot, tokens_ref.shape[0]).astype(BF16)
    used = used_column(counts_ref[...], peer_hot, most)
    gate = jnp.where(used, slot_column(gates_ref[...], peer_hot, k_hot), 0.0)
    copies[3].wait()
    out_ref[:, :width] = dot_nn(hot, tokens_ref[...]).astype(BF16)
    copies[4].wait()
    out_ref[:, width : 2 * width] = (dot_nn(hot, cot_ref[...]) * gate).astype(BF16)


def pack_matrix(flags):
    slots = flags.shape[0]
    before = (iota((slots, slots), 0) < iota((slots, slots), 1)).astype(BF16)
    same = (iota((slots, slots), 0) == iota((slots, slots), 1)).astype(BF16)
    place = dot_tn(flags, before)[:USED]
    used = dot_tn(flags, same)[:USED]
    row = iota((USED, slots), 0).astype(F32)
    return jnp.where(used > 0.5, jnp.where(place == row, 1.0, 0.0), 0.0).astype(BF16)


def pack_rows(arrived_ref, x_ref, pack_ref):
    width = x_ref.shape[1]
    size = jnp.max(jnp.abs(arrived_ref[:, width:]), axis=1, keepdims=True).astype(F32)
    flags = jnp.broadcast_to(jnp.where(size > 0.0, 1.0, 0.0), (arrived_ref.shape[0], LANES))
    pack = pack_matrix(flags.astype(BF16))
    pack_ref[...] = pack
    x_ref[...] = dot_nn(pack, arrived_ref[:, :width]).astype(BF16)


def own_hidden_grad(share, index_ref, arrived_ref, pack_ref, x_ref, w_down_ref, grad_ref, *refs):
    *load_refs, scaled_ref, own_ref, middle_ref, sems = refs
    inner, width = w_down_ref.shape
    copies = []
    if load_refs:
        own_hbm, near_ref, far_ref, middle_hbm = load_refs
        for place, target in enumerate((own_hbm, middle_hbm)):
            x_part = target.at[:, pl.ds(inner + share, width)]
            copies.append(pltpu.make_async_copy(x_ref, x_part, sems.at[place]))
            copies[-1].start()
    scaled_ref[...] = dot_nn(pack_ref[...], arrived_ref[:, width : 2 * width]).astype(BF16)
    hidden_grad = dot_nt(scaled_ref[...], w_down_ref[...])
    grad_ref[...] = hidden_grad
    if not load_refs:
        return
    for place, (load_ref, steps) in enumerate(zip((own_ref, middle_ref, near_ref, far_ref), LOADS)):
        load_ref[:, :inner] = hidden_grad.astype(BF16)
        for part, step in enumerate(steps):
            start = pl.multiple_of((index_ref[0] ^ step) * share, LANES)
            load_ref[:, pl.ds(inner + part * share, share)] = scaled_ref[:, pl.ds(start, share)]
        if place < 2:
            load_part = (own_hbm, middle_hbm)[place].at[:, pl.ds(0, inner + share)]
            copies.append(pltpu.make_async_copy(load_ref, load_part, sems.at[2 + place]))
            copies[-1].start()
    for copy in copies:
        copy.wait()


def activations(pre, inner):
    gate_pre = pre[:, :inner]
    up_pre = pre[:, inner:]
    squash = jax.nn.sigmoid(gate_pre)
    swished = gate_pre * squash
    hidden = (swished * up_pre).astype(BF16)
    return hidden, up_pre * (squash * (1.0 + gate_pre * (1.0 - squash))), swished


def start_parts(source, target, sems, parts=4):
    depth = source.shape[0] // parts
    copies = []
    for part in range(parts):
        span = pl.ds(part * depth, depth)
        copies.append(pltpu.make_async_copy(source.at[span], target.at[span], sems.at[part]))
        copies[-1].start()
    return copies


def project(x, w_ref, copies):
    depth = w_ref.shape[0] // len(copies)
    total = None
    for part, copy in enumerate(copies):
        copy.wait()
        span = slice(part * depth, (part + 1) * depth)
        term = dot_nn(x[:, span], w_ref[span, :])
        total = term if total is None else total + term
    return total


def own_rows(x_ref, grad_ref, pack_ref, w_in_hbm, out_ref, w_in_ref, sems):
    inner = grad_ref.shape[1]
    width = w_in_ref.shape[0]
    copies = start_parts(w_in_hbm, w_in_ref, sems)
    hidden_grad = grad_ref[...]
    hidden, gate_factor, up_factor = activations(project(x_ref, w_in_ref, copies), inner)
    gate_rows = (hidden_grad * gate_factor).astype(BF16)
    up_rows = (hidden_grad * up_factor).astype(BF16)
    value = jnp.sum(hidden.astype(F32) * hidden_grad, axis=1, keepdims=True)
    high = value.astype(BF16).astype(F32)
    low = value - high
    lane = iota((x_ref.shape[0], LANES), 1)
    tail = jnp.where(lane == 0, high, jnp.where(lane == 1, low, 0.0)).astype(BF16)
    slot_grad = (
        dot_nt(gate_rows, w_in_ref[:, :inner]) + dot_nt(up_rows, w_in_ref[:, inner:])
    ).astype(BF16)
    pack = pack_ref[...]
    out_ref[:, :width] = dot_tn(pack, slot_grad).astype(BF16)
    out_ref[:, width:] = dot_tn(pack, tail).astype(BF16)


def combine_tokens(rows_ref, counts_ref, gates_ref, back_ref, token_ref, gate_ref):
    peers, most = rows_ref.shape
    tokens, width = token_ref.shape
    peer_hot, k_hot = slot_maps(peers, most)
    hot = token_hot(rows_ref, peer_hot, k_hot, tokens)
    used = used_column(counts_ref[...], peer_hot, most)
    token_ref[...] = dot_tn(hot.astype(BF16), back_ref[:, :width]).astype(BF16)
    value = back_ref[:, width : width + 1].astype(F32) + back_ref[:, width + 1 : width + 2].astype(F32)
    gate = jnp.where(used, slot_column(gates_ref[...], peer_hot, k_hot), 1.0)
    value = jnp.where(used, value / gate, 0.0).astype(BF16).astype(F32)
    spread = jnp.where(k_hot, value, 0.0).astype(BF16)
    gate_ref[...] = dot_tn(peer_hot.astype(BF16), spread).astype(BF16)


def near_rows(share, *refs):
    x_refs, load_refs, index_ref, w_in_ref = refs[:2], refs[2:5], refs[5], refs[6]
    w_in_held, x_share_ref, s_share_ref, hidden_ref, in_rows_ref, held, sems = refs[7:]
    copies = start_parts(w_in_ref, w_in_held, sems)
    inner = hidden_ref.shape[1]
    held[:USED, :] = load_refs[0][:, inner + share :]
    for place, ref in enumerate(x_refs, 1):
        held[place * USED : (place + 1) * USED, :] = ref[...]
    x_share_ref[...] = held[:, pl.ds(pl.multiple_of(index_ref[0] * share, LANES), share)]
    hidden, gate_factor, up_factor = activations(project(held, w_in_held, copies), inner)
    hidden_ref[...] = hidden
    for place, ref in enumerate(load_refs):
        rows = slice(place * USED, (place + 1) * USED)
        grad = ref[:, :inner].astype(F32)
        in_rows_ref[rows, :inner] = (grad * gate_factor[rows]).astype(BF16)
        in_rows_ref[rows, inner:] = (grad * up_factor[rows]).astype(BF16)
        s_share_ref[rows, :] = ref[:, inner : inner + share]


def third_rows(
    share, middle_ref, onward_ref, index_ref, w_in_ref, x_share_ref, hidden_ref, gate_factor_ref, up_factor_ref, held
):
    inner = hidden_ref.shape[1]
    held[...] = middle_ref[:, inner + share :] + onward_ref[...]
    x_share_ref[...] = held[:, pl.ds(pl.multiple_of(index_ref[0] * share, LANES), share)]
    hidden, gate_factor, up_factor = activations(dot_nn(held[...], w_in_ref[...]), hidden_ref.shape[1])
    hidden_ref[...] = hidden
    gate_factor_ref[...] = gate_factor
    up_factor_ref[...] = up_factor


def grads(middle_ref, onward_ref, *refs):
    first, third = refs[:4], refs[4:8]
    in_hbm, down_hbm, x_share, s_share, hidden, in_rows, in_ref, down_ref, sems = refs[8:]
    inner, most, share = hidden.shape[1], 3 * USED, x_share.shape[1]
    for whole, part in zip((x_share, s_share, hidden, in_rows), first):
        whole[:most, :] = part[...]
    third_x_ref, third_hidden_ref, gate_factor_ref, up_factor_ref = third
    x_share[most:, :] = third_x_ref[...]
    hidden[most:, :] = third_hidden_ref[...]
    s_share[most:, :] = middle_ref[:, inner : inner + share] + onward_ref[:, inner + share :]
    grad = (middle_ref[:, :inner] + onward_ref[:, :inner]).astype(F32)
    copies = []
    for place, factor_ref in enumerate((gate_factor_ref, up_factor_ref)):
        half = pl.ds(place * inner, inner)
        in_rows[most:, half] = (grad * factor_ref[...]).astype(BF16)
        in_ref[:, half] = dot_tn(x_share[...], in_rows[:, half]).astype(BF16)
        copies.append(pltpu.make_async_copy(in_ref.at[:, half], in_hbm.at[:, half], sems.at[place]))
        copies[-1].start()
    down_ref[...] = dot_tn(hidden[...], s_share[...]).astype(BF16)
    copies.append(pltpu.make_async_copy(down_ref, down_hbm, sems.at[2]))
    copies[-1].start()
    for copy in copies:
        copy.wait()


def to_experts(block, peers):
    slots, width = block.shape
    moved = lax.all_to_all(
        block.reshape(peers, slots // peers, width), "expert", split_axis=0, concat_axis=0, tiled=True
    )
    return moved.reshape(slots, width)


def on_device(
    replicas, tokens, out_cotangent, chosen_rows, counts, gate_weights, in_weights, down_weights
):
    tokens, cot, w_in, w_down = tokens[0], out_cotangent[0], in_weights[0], down_weights[0]
    rows, count, gates = chosen_rows[0, 0], counts[0], gate_weights[0, 0]
    peers, most = rows.shape
    slots = peers * most
    n_tokens, width = tokens.shape
    inner = w_down.shape[0]
    share = width // replicas
    on_line = replicas == 4 and share % LANES == 0
    index = lax.axis_index("dp").astype(jnp.int32).reshape(1)
    shape = jax.ShapeDtypeStruct
    vmem = pl.BlockSpec(memory_space=pltpu.VMEM)
    smem = pl.BlockSpec(memory_space=pltpu.SMEM)
    hbm = pl.BlockSpec(memory_space=pltpu.HBM)

    w_in_far = pltpu.with_memory_space_constraint(w_in, pltpu.HBM)
    picked = (rows, count, gates, tokens, cot)
    (sent,) = call(
        pick_rows,
        [shape((slots, 2 * width), BF16)],
        [pltpu.with_memory_space_constraint(a, pltpu.HBM) for a in picked],
        4 * slots * n_tokens * width,
        [hbm] * 5,
        [pltpu.VMEM(a.shape, a.dtype) for a in picked] + [pltpu.SemaphoreType.DMA((5,))],
        8,
    )
    arrived = to_experts(sent, peers)
    x_rows, pack = call(
        pack_rows,
        [shape((USED, width), BF16), shape((USED, slots), BF16)],
        (arrived,),
        2 * USED * slots * width,
        vmem=6,
    )
    short = inner + share
    hidden_grad, *loads = call(
        functools.partial(own_hidden_grad, share),
        [shape((USED, inner), F32)]
        + [
            pltpu.HBM((USED, short + width), BF16),
            shape((USED, short), BF16),
            shape((USED, short + share), BF16),
            pltpu.HBM((USED, short + width), BF16),
        ]
        * on_line,
        (index, arrived, pack, x_rows, w_down),
        2 * USED * width * (slots + inner),
        [smem] + [vmem] * 4,
        [
            pltpu.VMEM((USED, width), BF16),
            pltpu.VMEM((USED, short), BF16),
            pltpu.VMEM((USED, short), BF16),
            pltpu.SemaphoreType.DMA((4,)),
        ],
        8,
        [vmem] + [hbm, vmem, vmem, hbm] * on_line,
    )
    if on_line:
        own, near_load, far_load, middle_load = loads
        x_far = lax.ppermute(x_rows, "dp", FAR)
        x_near = lax.ppermute(x_rows, "dp", NEAR)
        near = lax.ppermute(near_load, "dp", NEAR)
    parts = 4
    (sent_back,) = call(
        own_rows,
        [shape((slots, width + LANES), BF16)],
        (x_rows, hidden_grad, pack, w_in_far),
        2 * USED * inner * width * 4,
        [vmem] * 3 + [hbm],
        [pltpu.VMEM(w_in.shape, BF16), pltpu.SemaphoreType.DMA((parts,))],
        16,
    )
    if on_line:
        far_load, sent_back = lax.optimization_barrier((far_load, sent_back))
        far = lax.ppermute(far_load, "dp", FAR)
        x_near, near, x_far, sent_back = lax.optimization_barrier((x_near, near, x_far, sent_back))
    back = to_experts(sent_back, peers)
    if on_line:
        middle = lax.ppermute(middle_load, "dp", MIDDLE)
        x_onward = lax.ppermute(x_far, "dp", ONWARD)
        onward = lax.ppermute(far, "dp", ONWARD)
    token_grad, gate_grad = call(
        combine_tokens,
        [shape((n_tokens, width), BF16), shape((peers, most), BF16)],
        (rows, count, gates, back),
        2 * slots * n_tokens * width,
        vmem=8,
    )
    if on_line:
        everyone, first = replicas * USED, 3 * USED

        w_in_held, *first_parts = call(
            functools.partial(near_rows, share),
            [
                shape(w_in.shape, BF16),
                shape((first, share), BF16),
                shape((first, share), BF16),
                shape((first, inner), BF16),
                shape((first, 2 * inner), BF16),
            ],
            (x_near, x_far, own, near, far, index, w_in_far),
            4 * first * inner * width,
            [vmem] * 5 + [smem, hbm],
            [pltpu.VMEM((first, width), BF16), pltpu.SemaphoreType.DMA((parts,))],
            16,
        )
        third_parts = call(
            functools.partial(third_rows, share),
            [
                shape((USED, share), BF16),
                shape((USED, inner), BF16),
                shape((USED, inner), F32),
                shape((USED, inner), F32),
            ],
            (middle, x_onward, index, w_in_held),
            4 * USED * inner * width,
            [vmem] * 2 + [smem, vmem],
            [pltpu.VMEM((USED, width), BF16)],
            16,
        )
        middle, token_grad = lax.optimization_barrier((middle, token_grad))
        in_grad, down_grad = call(
            grads,
            [shape((share, 2 * inner), BF16), shape((inner, share), BF16)],
            (middle, onward, *first_parts, *third_parts),
            6 * everyone * inner * share,
            None,
            [
                pltpu.VMEM((everyone, share), BF16),
                pltpu.VMEM((everyone, share), BF16),
                pltpu.VMEM((everyone, inner), BF16),
                pltpu.VMEM((everyone, 2 * inner), BF16),
                pltpu.VMEM((share, 2 * inner), BF16),
                pltpu.VMEM((inner, share), BF16),
                pltpu.SemaphoreType.DMA((3,)),
            ],
            16,
            [hbm] * 2,
        )
    else:
        x_all = lax.all_gather(x_rows, "dp", axis=0, tiled=True)
        hidden, gate_factor, up_factor = activations(dot_nn(x_all, w_in), inner)
        hidden_grad = lax.all_gather(hidden_grad, "dp", axis=0, tiled=True)
        in_rows = jnp.concatenate([hidden_grad * gate_factor, hidden_grad * up_factor], axis=1)
        x_share = lax.dynamic_slice_in_dim(x_all, index[0] * share, share, axis=1)
        scaled = dot_nn(pack, arrived[:, width : 2 * width]).astype(BF16)
        s_all = lax.all_gather(scaled, "dp", axis=0, tiled=True)
        s_share = lax.dynamic_slice_in_dim(s_all, index[0] * share, share, axis=1)
        in_grad = dot_tn(x_share, in_rows.astype(BF16)).astype(BF16)
        down_grad = dot_tn(hidden, s_share).astype(BF16)
    return (token_grad[None], gate_grad[None, None], in_grad[None], down_grad[None])


def solution(mesh):
    return jax.shard_map(
        functools.partial(on_device, mesh.shape["dp"]),
        mesh=mesh,
        in_specs=(
            P("dp", "expert", None),
            P("dp", "expert", None),
            P("dp", "expert", None, None),
            P("dp", "expert", None),
            P("dp", "expert", None, None),
            P("expert", None, None),
            P("expert", None, None),
        ),
        out_specs=(
            P("dp", "expert", None),
            P("dp", "expert", None, None),
            P("expert", "dp", None),
            P("expert", None, "dp"),
        ),
        check_vma=False,
    )
```

```python
import functools
import math

import jax
import jax.numpy as jnp
from jax import lax
from jax.experimental import pallas as pl
from jax.experimental.pallas import tpu as pltpu
from jax.sharding import PartitionSpec as P

F32 = jnp.float32
BF16 = jnp.bfloat16
USED = 64
LANES = 128

NEAR = ((0, 1), (1, 0), (2, 3), (3, 2))
MIDDLE = ((1, 2), (2, 1))
FAR = ((0, 2), (2, 0), (1, 3), (3, 1))
ONWARD = ((1, 0), (2, 3))
LOADS = ((0,), (3,), (1,), (2, 3))


def dot_nn(left, right):
    return lax.dot_general(left, right, (((1,), (0,)), ((), ())), preferred_element_type=F32)


def dot_nt(left, right):
    return lax.dot_general(left, right, (((1,), (1,)), ((), ())), preferred_element_type=F32)


def dot_tn(left, right):
    return lax.dot_general(left, right, (((0,), (0,)), ((), ())), preferred_element_type=F32)


def iota(shape, dim):
    return lax.broadcasted_iota(jnp.int32, shape, dim)


def call(body, outs, args, flops, in_specs=None, scratch=(), vmem=24, out_specs=None):
    size = sum(math.prod(a.shape) * a.dtype.itemsize for a in (*args, *outs))
    return pl.pallas_call(
        body,
        out_shape=tuple(outs),
        in_specs=in_specs or [pl.BlockSpec(memory_space=pltpu.VMEM)] * len(args),
        out_specs=tuple(out_specs or [pl.BlockSpec(memory_space=pltpu.VMEM) for _ in outs]),
        scratch_shapes=scratch,
        compiler_params=pltpu.CompilerParams(vmem_limit_bytes=vmem * 1024 * 1024),
        cost_estimate=pl.CostEstimate(flops=int(flops), bytes_accessed=int(size), transcendentals=0),
    )(*args)


def slot_maps(peers, most):
    slots = peers * most
    peer_hot = iota((slots, peers), 0) // most == iota((slots, peers), 1)
    k_hot = iota((slots, most), 0) % most == iota((slots, most), 1)
    return peer_hot, k_hot


def slot_column(values, peer_hot, k_hot):
    spread = dot_nn(peer_hot.astype(BF16), values)
    return jnp.sum(jnp.where(k_hot, spread, 0.0), axis=1, keepdims=True)


def token_hot(rows_ref, peer_hot, k_hot, tokens):
    column = slot_column(rows_ref[...].astype(F32).astype(BF16), peer_hot, k_hot)
    return iota((column.shape[0], tokens), 1) == column.astype(jnp.int32)


def used_column(counts, peer_hot, most):
    slots = peer_hot.shape[0]
    count = jnp.sum(jnp.where(peer_hot, counts.astype(F32), 0.0), axis=1, keepdims=True)
    return (iota((slots, 1), 0) % most).astype(F32) < count


def pick_rows(*refs):
    sources, out_ref, held, sems = refs[:5], refs[5], refs[6:11], refs[11]
    copies = [
        pltpu.make_async_copy(source, target, sems.at[place])
        for place, (source, target) in enumerate(zip(sources, held))
    ]
    for copy in copies:
        copy.start()
    rows_ref, counts_ref, gates_ref, tokens_ref, cot_ref = held
    peers, most = rows_ref.shape
    slots = peers * most
    width = tokens_ref.shape[1]
    peer_hot, k_hot = slot_maps(peers, most)
    for copy in copies[:3]:
        copy.wait()
    hot = token_hot(rows_ref, peer_hot, k_hot, tokens_ref.shape[0]).astype(BF16)
    used = used_column(counts_ref[...], peer_hot, most)
    gate = jnp.where(used, slot_column(gates_ref[...], peer_hot, k_hot), 0.0)
    copies[3].wait()
    out_ref[:, :width] = dot_nn(hot, tokens_ref[...]).astype(BF16)
    copies[4].wait()
    out_ref[:, width : 2 * width] = (dot_nn(hot, cot_ref[...]) * gate).astype(BF16)


def pack_matrix(flags):
    slots = flags.shape[0]
    before = (iota((slots, slots), 0) < iota((slots, slots), 1)).astype(BF16)
    same = (iota((slots, slots), 0) == iota((slots, slots), 1)).astype(BF16)
    place = dot_tn(flags, before)[:USED]
    used = dot_tn(flags, same)[:USED]
    row = iota((USED, slots), 0).astype(F32)
    return jnp.where(used > 0.5, jnp.where(place == row, 1.0, 0.0), 0.0).astype(BF16)


def pack_rows(arrived_ref, x_ref, pack_ref):
    width = x_ref.shape[1]
    size = jnp.max(jnp.abs(arrived_ref[:, width:]), axis=1, keepdims=True).astype(F32)
    flags = jnp.broadcast_to(jnp.where(size > 0.0, 1.0, 0.0), (arrived_ref.shape[0], LANES))
    pack = pack_matrix(flags.astype(BF16))
    pack_ref[...] = pack
    x_ref[...] = dot_nn(pack, arrived_ref[:, :width]).astype(BF16)


def own_hidden_grad(share, index_ref, arrived_ref, pack_ref, _, w_down_ref, grad_ref, *refs):
    *load_refs, scaled_ref = refs
    inner, width = w_down_ref.shape
    scaled_ref[...] = dot_nn(pack_ref[...], arrived_ref[:, width : 2 * width]).astype(BF16)
    hidden_grad = dot_nt(scaled_ref[...], w_down_ref[...])
    grad_ref[...] = hidden_grad
    for load_ref, steps in zip(load_refs, LOADS):
        load_ref[:, :inner] = hidden_grad.astype(BF16)
        for part, step in enumerate(steps):
            start = pl.multiple_of((index_ref[0] ^ step) * share, LANES)
            load_ref[:, pl.ds(inner + part * share, share)] = scaled_ref[:, pl.ds(start, share)]


def activations(pre, inner):
    gate_pre = pre[:, :inner]
    up_pre = pre[:, inner:]
    squash = jax.nn.sigmoid(gate_pre)
    swished = gate_pre * squash
    hidden = (swished * up_pre).astype(BF16)
    return hidden, up_pre * (squash * (1.0 + gate_pre * (1.0 - squash))), swished


def start_parts(source, target, sems, parts=4):
    depth = source.shape[0] // parts
    copies = []
    for part in range(parts):
        span = pl.ds(part * depth, depth)
        copies.append(pltpu.make_async_copy(source.at[span], target.at[span], sems.at[part]))
        copies[-1].start()
    return copies


def project(x, w_ref, copies):
    depth = w_ref.shape[0] // len(copies)
    total = None
    for part, copy in enumerate(copies):
        copy.wait()
        span = slice(part * depth, (part + 1) * depth)
        term = dot_nn(x[:, span], w_ref[span, :])
        total = term if total is None else total + term
    return total


def own_rows(x_ref, grad_ref, pack_ref, w_in_hbm, *refs):
    *load_refs, w_in_ref, sems, load_sems = refs
    count = len(load_refs) // 2
    out_ref = load_refs[count]
    inner = grad_ref.shape[1]
    width = w_in_ref.shape[0]
    copies = start_parts(w_in_hbm, w_in_ref, sems)
    moves = []
    for load_ref, target in zip(load_refs[:count], load_refs[count + 1 :]):
        size = load_ref.shape[1]
        for source, span in ((load_ref, pl.ds(0, size)), (x_ref, pl.ds(size, width))):
            moves.append(pltpu.make_async_copy(source, target.at[:, span], load_sems.at[len(moves)]))
            moves[-1].start()
    hidden_grad = grad_ref[...]
    hidden, gate_factor, up_factor = activations(project(x_ref, w_in_ref, copies), inner)
    gate_rows = (hidden_grad * gate_factor).astype(BF16)
    up_rows = (hidden_grad * up_factor).astype(BF16)
    value = jnp.sum(hidden.astype(F32) * hidden_grad, axis=1, keepdims=True)
    high = value.astype(BF16).astype(F32)
    low = value - high
    lane = iota((x_ref.shape[0], LANES), 1)
    tail = jnp.where(lane == 0, high, jnp.where(lane == 1, low, 0.0)).astype(BF16)
    slot_grad = (
        dot_nt(gate_rows, w_in_ref[:, :inner]) + dot_nt(up_rows, w_in_ref[:, inner:])
    ).astype(BF16)
    pack = pack_ref[...]
    out_ref[:, :width] = dot_tn(pack, slot_grad).astype(BF16)
    out_ref[:, width:] = dot_tn(pack, tail).astype(BF16)
    for move in moves:
        move.wait()


def combine_tokens(rows_ref, counts_ref, gates_ref, back_ref, token_ref, gate_ref):
    peers, most = rows_ref.shape
    tokens, width = token_ref.shape
    peer_hot, k_hot = slot_maps(peers, most)
    hot = token_hot(rows_ref, peer_hot, k_hot, tokens)
    used = used_column(counts_ref[...], peer_hot, most)
    token_ref[...] = dot_tn(hot.astype(BF16), back_ref[:, :width]).astype(BF16)
    value = back_ref[:, width : width + 1].astype(F32) + back_ref[:, width + 1 : width + 2].astype(F32)
    gate = jnp.where(used, slot_column(gates_ref[...], peer_hot, k_hot), 1.0)
    value = jnp.where(used, value / gate, 0.0).astype(BF16).astype(F32)
    spread = jnp.where(k_hot, value, 0.0).astype(BF16)
    gate_ref[...] = dot_tn(peer_hot.astype(BF16), spread).astype(BF16)


def near_rows(share, *refs):
    x_refs, load_refs, index_ref, w_in_ref = refs[:2], refs[2:5], refs[5], refs[6]
    w_in_held, x_share_ref, s_share_ref, hidden_ref, in_rows_ref, held, sems = refs[7:]
    copies = start_parts(w_in_ref, w_in_held, sems)
    inner = hidden_ref.shape[1]
    held[:USED, :] = load_refs[0][:, inner + share :]
    for place, ref in enumerate(x_refs, 1):
        held[place * USED : (place + 1) * USED, :] = ref[...]
    x_share_ref[...] = held[:, pl.ds(pl.multiple_of(index_ref[0] * share, LANES), share)]
    hidden, gate_factor, up_factor = activations(project(held, w_in_held, copies), inner)
    hidden_ref[...] = hidden
    for place, ref in enumerate(load_refs):
        rows = slice(place * USED, (place + 1) * USED)
        grad = ref[:, :inner].astype(F32)
        in_rows_ref[rows, :inner] = (grad * gate_factor[rows]).astype(BF16)
        in_rows_ref[rows, inner:] = (grad * up_factor[rows]).astype(BF16)
        s_share_ref[rows, :] = ref[:, inner : inner + share]


def third_rows(
    share, middle_ref, onward_ref, index_ref, w_in_ref, x_share_ref, hidden_ref, gate_factor_ref, up_factor_ref, held
):
    inner = hidden_ref.shape[1]
    held[...] = middle_ref[:, inner + share :] + onward_ref[...]
    x_share_ref[...] = held[:, pl.ds(pl.multiple_of(index_ref[0] * share, LANES), share)]
    hidden, gate_factor, up_factor = activations(dot_nn(held[...], w_in_ref[...]), hidden_ref.shape[1])
    hidden_ref[...] = hidden
    gate_factor_ref[...] = gate_factor
    up_factor_ref[...] = up_factor


def grads(middle_ref, onward_ref, *refs):
    first, third = refs[:4], refs[4:8]
    in_hbm, down_hbm, x_share, s_share, hidden, in_rows, in_ref, down_ref, sems = refs[8:]
    inner, most, share = hidden.shape[1], 3 * USED, x_share.shape[1]
    for whole, part in zip((x_share, s_share, hidden, in_rows), first):
        whole[:most, :] = part[...]
    third_x_ref, third_hidden_ref, gate_factor_ref, up_factor_ref = third
    x_share[most:, :] = third_x_ref[...]
    hidden[most:, :] = third_hidden_ref[...]
    s_share[most:, :] = middle_ref[:, inner : inner + share] + onward_ref[:, inner + share :]
    grad = (middle_ref[:, :inner] + onward_ref[:, :inner]).astype(F32)
    copies = []
    for place, factor_ref in enumerate((gate_factor_ref, up_factor_ref)):
        half = pl.ds(place * inner, inner)
        in_rows[most:, half] = (grad * factor_ref[...]).astype(BF16)
        in_ref[:, half] = dot_tn(x_share[...], in_rows[:, half]).astype(BF16)
        copies.append(pltpu.make_async_copy(in_ref.at[:, half], in_hbm.at[:, half], sems.at[place]))
        copies[-1].start()
    down_ref[...] = dot_tn(hidden[...], s_share[...]).astype(BF16)
    copies.append(pltpu.make_async_copy(down_ref, down_hbm, sems.at[2]))
    copies[-1].start()
    for copy in copies:
        copy.wait()


def to_experts(block, peers):
    slots, width = block.shape
    moved = lax.all_to_all(
        block.reshape(peers, slots // peers, width), "expert", split_axis=0, concat_axis=0, tiled=True
    )
    return moved.reshape(slots, width)


def on_device(
    replicas, tokens, out_cotangent, chosen_rows, counts, gate_weights, in_weights, down_weights
):
    tokens, cot, w_in, w_down = tokens[0], out_cotangent[0], in_weights[0], down_weights[0]
    rows, count, gates = chosen_rows[0, 0], counts[0], gate_weights[0, 0]
    peers, most = rows.shape
    slots = peers * most
    n_tokens, width = tokens.shape
    inner = w_down.shape[0]
    share = width // replicas
    on_line = replicas == 4 and share % LANES == 0
    index = lax.axis_index("dp").astype(jnp.int32).reshape(1)
    shape = jax.ShapeDtypeStruct
    vmem = pl.BlockSpec(memory_space=pltpu.VMEM)
    smem = pl.BlockSpec(memory_space=pltpu.SMEM)
    hbm = pl.BlockSpec(memory_space=pltpu.HBM)

    w_in_far = pltpu.with_memory_space_constraint(w_in, pltpu.HBM)
    picked = (rows, count, gates, tokens, cot)
    (sent,) = call(
        pick_rows,
        [shape((slots, 2 * width), BF16)],
        [pltpu.with_memory_space_constraint(a, pltpu.HBM) for a in picked],
        4 * slots * n_tokens * width,
        [hbm] * 5,
        [pltpu.VMEM(a.shape, a.dtype) for a in picked] + [pltpu.SemaphoreType.DMA((5,))],
        8,
    )
    arrived = to_experts(sent, peers)
    x_rows, pack = call(
        pack_rows,
        [shape((USED, width), BF16), shape((USED, slots), BF16)],
        (arrived,),
        2 * USED * slots * width,
        vmem=6,
    )
    short = inner + share
    hidden_grad, *loads = call(
        functools.partial(own_hidden_grad, share),
        [shape((USED, inner), F32)]
        + [
            shape((USED, short), BF16),
            shape((USED, short), BF16),
            shape((USED, short), BF16),
            shape((USED, short + share), BF16),
        ]
        * on_line,
        (index, arrived, pack, x_rows, w_down),
        2 * USED * width * (slots + inner),
        [smem] + [vmem] * 4,
        [
            pltpu.VMEM((USED, width), BF16),
        ],
        8,
    )
    if on_line:
        own, middle_load, near_load, far_load = loads
        x_far = lax.ppermute(x_rows, "dp", FAR)
        x_near = lax.ppermute(x_rows, "dp", NEAR)
        near = lax.ppermute(near_load, "dp", NEAR)
    parts = 4
    sent_back, *loads = call(
        own_rows,
        [shape((slots, width + LANES), BF16)] + [pltpu.HBM((USED, short + width), BF16)] * 2 * on_line,
        (x_rows, hidden_grad, pack, w_in_far, *loads[:2]),
        2 * USED * inner * width * 4,
        [vmem] * 3 + [hbm] + [vmem] * 2 * on_line,
        [pltpu.VMEM(w_in.shape, BF16), pltpu.SemaphoreType.DMA((parts,)), pltpu.SemaphoreType.DMA((4,))],
        16,
        [vmem] + [hbm] * 2 * on_line,
    )
    if on_line:
        own, middle_load = loads
    if on_line:
        far = lax.ppermute(far_load, "dp", FAR)
        x_near, x_far, sent_back = lax.optimization_barrier((x_near, x_far, sent_back))
    back = to_experts(sent_back, peers)
    if on_line:
        middle_load, near, sent_back = lax.optimization_barrier((middle_load, near, sent_back))
        middle = lax.ppermute(middle_load, "dp", MIDDLE)
        x_onward = lax.ppermute(x_far, "dp", ONWARD)
        onward = lax.ppermute(far, "dp", ONWARD)
    token_grad, gate_grad = call(
        combine_tokens,
        [shape((n_tokens, width), BF16), shape((peers, most), BF16)],
        (rows, count, gates, back),
        2 * slots * n_tokens * width,
        vmem=8,
    )
    if on_line:
        everyone, first = replicas * USED, 3 * USED

        w_in_held, *first_parts = call(
            functools.partial(near_rows, share),
            [
                shape(w_in.shape, BF16),
                shape((first, share), BF16),
                shape((first, share), BF16),
                shape((first, inner), BF16),
                shape((first, 2 * inner), BF16),
            ],
            (x_near, x_far, own, near, far, index, w_in_far),
            4 * first * inner * width,
            [vmem] * 5 + [smem, hbm],
            [pltpu.VMEM((first, width), BF16), pltpu.SemaphoreType.DMA((parts,))],
            16,
        )
        third_parts = call(
            functools.partial(third_rows, share),
            [
                shape((USED, share), BF16),
                shape((USED, inner), BF16),
                shape((USED, inner), F32),
                shape((USED, inner), F32),
            ],
            (middle, x_onward, index, w_in_held),
            4 * USED * inner * width,
            [vmem] * 2 + [smem, vmem],
            [pltpu.VMEM((USED, width), BF16)],
            16,
        )
        middle, token_grad = lax.optimization_barrier((middle, token_grad))
        in_grad, down_grad = call(
            grads,
            [shape((share, 2 * inner), BF16), shape((inner, share), BF16)],
            (middle, onward, *first_parts, *third_parts),
            6 * everyone * inner * share,
            None,
            [
                pltpu.VMEM((everyone, share), BF16),
                pltpu.VMEM((everyone, share), BF16),
                pltpu.VMEM((everyone, inner), BF16),
                pltpu.VMEM((everyone, 2 * inner), BF16),
                pltpu.VMEM((share, 2 * inner), BF16),
                pltpu.VMEM((inner, share), BF16),
                pltpu.SemaphoreType.DMA((3,)),
            ],
            16,
            [hbm] * 2,
        )
    else:
        x_all = lax.all_gather(x_rows, "dp", axis=0, tiled=True)
        hidden, gate_factor, up_factor = activations(dot_nn(x_all, w_in), inner)
        hidden_grad = lax.all_gather(hidden_grad, "dp", axis=0, tiled=True)
        in_rows = jnp.concatenate([hidden_grad * gate_factor, hidden_grad * up_factor], axis=1)
        x_share = lax.dynamic_slice_in_dim(x_all, index[0] * share, share, axis=1)
        scaled = dot_nn(pack, arrived[:, width : 2 * width]).astype(BF16)
        s_all = lax.all_gather(scaled, "dp", axis=0, tiled=True)
        s_share = lax.dynamic_slice_in_dim(s_all, index[0] * share, share, axis=1)
        in_grad = dot_tn(x_share, in_rows.astype(BF16)).astype(BF16)
        down_grad = dot_tn(hidden, s_share).astype(BF16)
    return (token_grad[None], gate_grad[None, None], in_grad[None], down_grad[None])


def solution(mesh):
    return jax.shard_map(
        functools.partial(on_device, mesh.shape["dp"]),
        mesh=mesh,
        in_specs=(
            P("dp", "expert", None),
            P("dp", "expert", None),
            P("dp", "expert", None, None),
            P("dp", "expert", None),
            P("dp", "expert", None, None),
            P("expert", None, None),
            P("expert", None, None),
        ),
        out_specs=(
            P("dp", "expert", None),
            P("dp", "expert", None, None),
            P("expert", "dp", None),
            P("expert", None, "dp"),
        ),
        check_vma=False,
    )
```

```python
import functools
import math

import jax
import jax.numpy as jnp
from jax import lax
from jax.experimental import pallas as pl
from jax.experimental.pallas import tpu as pltpu
from jax.sharding import PartitionSpec as P

F32 = jnp.float32
BF16 = jnp.bfloat16
USED = 64
LANES = 128

NEAR = ((0, 1), (1, 0), (2, 3), (3, 2))
MIDDLE = ((1, 2), (2, 1))
FAR = ((0, 2), (2, 0), (1, 3), (3, 1))
ONWARD = ((1, 0), (2, 3))
LOADS = ((0,), (3,), (1,), (2, 3))


def dot_nn(left, right):
    return lax.dot_general(left, right, (((1,), (0,)), ((), ())), preferred_element_type=F32)


def dot_nt(left, right):
    return lax.dot_general(left, right, (((1,), (1,)), ((), ())), preferred_element_type=F32)


def dot_tn(left, right):
    return lax.dot_general(left, right, (((0,), (0,)), ((), ())), preferred_element_type=F32)


def iota(shape, dim):
    return lax.broadcasted_iota(jnp.int32, shape, dim)


def call(body, outs, args, flops, in_specs=None, scratch=(), vmem=24, out_specs=None):
    size = sum(math.prod(a.shape) * a.dtype.itemsize for a in (*args, *outs))
    return pl.pallas_call(
        body,
        out_shape=tuple(outs),
        in_specs=in_specs or [pl.BlockSpec(memory_space=pltpu.VMEM)] * len(args),
        out_specs=tuple(out_specs or [pl.BlockSpec(memory_space=pltpu.VMEM) for _ in outs]),
        scratch_shapes=scratch,
        compiler_params=pltpu.CompilerParams(vmem_limit_bytes=vmem * 1024 * 1024),
        cost_estimate=pl.CostEstimate(flops=int(flops), bytes_accessed=int(size), transcendentals=0),
    )(*args)


def slot_maps(peers, most):
    slots = peers * most
    peer_hot = iota((slots, peers), 0) // most == iota((slots, peers), 1)
    k_hot = iota((slots, most), 0) % most == iota((slots, most), 1)
    return peer_hot, k_hot


def slot_column(values, peer_hot, k_hot):
    spread = dot_nn(peer_hot.astype(BF16), values)
    return jnp.sum(jnp.where(k_hot, spread, 0.0), axis=1, keepdims=True)


def token_hot(rows_ref, peer_hot, k_hot, tokens):
    column = slot_column(rows_ref[...].astype(F32).astype(BF16), peer_hot, k_hot)
    return iota((column.shape[0], tokens), 1) == column.astype(jnp.int32)


def used_column(counts, peer_hot, most):
    slots = peer_hot.shape[0]
    count = jnp.sum(jnp.where(peer_hot, counts.astype(F32), 0.0), axis=1, keepdims=True)
    return (iota((slots, 1), 0) % most).astype(F32) < count


def pick_rows(*refs):
    sources, gates_ref, out_ref, held, sems = refs[:4], refs[4], refs[5], refs[6:10], refs[10]
    copies = [
        pltpu.make_async_copy(source, target, sems.at[place])
        for place, (source, target) in enumerate(zip(sources, held))
    ]
    for copy in copies:
        copy.start()
    rows_ref, counts_ref, tokens_ref, cot_ref = held
    peers, most = rows_ref.shape
    slots = peers * most
    width = tokens_ref.shape[1]
    peer_hot, k_hot = slot_maps(peers, most)
    for copy in copies[:2]:
        copy.wait()
    hot = token_hot(rows_ref, peer_hot, k_hot, tokens_ref.shape[0]).astype(BF16)
    used = used_column(counts_ref[...], peer_hot, most)
    gate = jnp.where(used, slot_column(gates_ref[...], peer_hot, k_hot), 0.0)
    copies[2].wait()
    out_ref[:, :width] = dot_nn(hot, tokens_ref[...]).astype(BF16)
    copies[3].wait()
    out_ref[:, width : 2 * width] = (dot_nn(hot, cot_ref[...]) * gate).astype(BF16)


def pack_matrix(flags):
    slots = flags.shape[0]
    before = (iota((slots, slots), 0) < iota((slots, slots), 1)).astype(BF16)
    same = (iota((slots, slots), 0) == iota((slots, slots), 1)).astype(BF16)
    place = dot_tn(flags, before)[:USED]
    used = dot_tn(flags, same)[:USED]
    row = iota((USED, slots), 0).astype(F32)
    return jnp.where(used > 0.5, jnp.where(place == row, 1.0, 0.0), 0.0).astype(BF16)


def pack_rows(arrived_ref, x_ref, pack_ref):
    width = x_ref.shape[1]
    size = jnp.max(jnp.abs(arrived_ref[:, width:]), axis=1, keepdims=True).astype(F32)
    flags = jnp.broadcast_to(jnp.where(size > 0.0, 1.0, 0.0), (arrived_ref.shape[0], LANES))
    pack = pack_matrix(flags.astype(BF16))
    pack_ref[...] = pack
    x_ref[...] = dot_nn(pack, arrived_ref[:, :width]).astype(BF16)


def own_hidden_grad(share, index_ref, arrived_ref, pack_ref, _, w_down_ref, grad_ref, *refs):
    *load_refs, scaled_ref = refs
    inner, width = w_down_ref.shape
    scaled_ref[...] = dot_nn(pack_ref[...], arrived_ref[:, width : 2 * width]).astype(BF16)
    hidden_grad = dot_nt(scaled_ref[...], w_down_ref[...])
    grad_ref[...] = hidden_grad
    for load_ref, steps in zip(load_refs, LOADS):
        load_ref[:, :inner] = hidden_grad.astype(BF16)
        for part, step in enumerate(steps):
            start = pl.multiple_of((index_ref[0] ^ step) * share, LANES)
            load_ref[:, pl.ds(inner + part * share, share)] = scaled_ref[:, pl.ds(start, share)]


def activations(pre, inner):
    gate_pre = pre[:, :inner]
    up_pre = pre[:, inner:]
    squash = jax.nn.sigmoid(gate_pre)
    swished = gate_pre * squash
    hidden = (swished * up_pre).astype(BF16)
    return hidden, up_pre * (squash * (1.0 + gate_pre * (1.0 - squash))), swished


def start_parts(source, target, sems, parts=4):
    depth = source.shape[0] // parts
    copies = []
    for part in range(parts):
        span = pl.ds(part * depth, depth)
        copies.append(pltpu.make_async_copy(source.at[span], target.at[span], sems.at[part]))
        copies[-1].start()
    return copies


def project(x, w_ref, copies):
    depth = w_ref.shape[0] // len(copies)
    total = None
    for part, copy in enumerate(copies):
        copy.wait()
        span = slice(part * depth, (part + 1) * depth)
        term = dot_nn(x[:, span], w_ref[span, :])
        total = term if total is None else total + term
    return total


def own_rows(x_ref, grad_ref, pack_ref, w_in_hbm, *refs):
    *load_refs, w_in_ref, sems, load_sems = refs
    count = len(load_refs) // 2
    out_ref = load_refs[count]
    inner = grad_ref.shape[1]
    width = w_in_ref.shape[0]
    copies = start_parts(w_in_hbm, w_in_ref, sems)
    moves = []
    for load_ref, target in zip(load_refs[:count], load_refs[count + 1 :]):
        size = load_ref.shape[1]
        for source, span in ((load_ref, pl.ds(0, size)), (x_ref, pl.ds(size, width))):
            moves.append(pltpu.make_async_copy(source, target.at[:, span], load_sems.at[len(moves)]))
            moves[-1].start()
    hidden_grad = grad_ref[...]
    hidden, gate_factor, up_factor = activations(project(x_ref, w_in_ref, copies), inner)
    gate_rows = (hidden_grad * gate_factor).astype(BF16)
    up_rows = (hidden_grad * up_factor).astype(BF16)
    value = jnp.sum(hidden.astype(F32) * hidden_grad, axis=1, keepdims=True)
    high = value.astype(BF16).astype(F32)
    low = value - high
    lane = iota((x_ref.shape[0], LANES), 1)
    tail = jnp.where(lane == 0, high, jnp.where(lane == 1, low, 0.0)).astype(BF16)
    slot_grad = (
        dot_nt(gate_rows, w_in_ref[:, :inner]) + dot_nt(up_rows, w_in_ref[:, inner:])
    ).astype(BF16)
    pack = pack_ref[...]
    out_ref[:, :width] = dot_tn(pack, slot_grad).astype(BF16)
    out_ref[:, width:] = dot_tn(pack, tail).astype(BF16)
    for move in moves:
        move.wait()


def combine_tokens(rows_ref, counts_ref, gates_ref, back_ref, token_ref, gate_ref):
    peers, most = rows_ref.shape
    tokens, width = token_ref.shape
    peer_hot, k_hot = slot_maps(peers, most)
    hot = token_hot(rows_ref, peer_hot, k_hot, tokens)
    used = used_column(counts_ref[...], peer_hot, most)
    token_ref[...] = dot_tn(hot.astype(BF16), back_ref[:, :width]).astype(BF16)
    value = back_ref[:, width : width + 1].astype(F32) + back_ref[:, width + 1 : width + 2].astype(F32)
    gate = jnp.where(used, slot_column(gates_ref[...], peer_hot, k_hot), 1.0)
    value = jnp.where(used, value / gate, 0.0).astype(BF16).astype(F32)
    spread = jnp.where(k_hot, value, 0.0).astype(BF16)
    gate_ref[...] = dot_tn(peer_hot.astype(BF16), spread).astype(BF16)


def near_rows(share, *refs):
    x_refs, load_refs, index_ref, w_in_ref = refs[:2], refs[2:5], refs[5], refs[6]
    w_in_held, x_share_ref, s_share_ref, hidden_ref, in_rows_ref, held, sems = refs[7:]
    copies = start_parts(w_in_ref, w_in_held, sems)
    inner = hidden_ref.shape[1]
    held[:USED, :] = load_refs[0][:, inner + share :]
    for place, ref in enumerate(x_refs, 1):
        held[place * USED : (place + 1) * USED, :] = ref[...]
    x_share_ref[...] = held[:, pl.ds(pl.multiple_of(index_ref[0] * share, LANES), share)]
    hidden, gate_factor, up_factor = activations(project(held, w_in_held, copies), inner)
    hidden_ref[...] = hidden
    for place, ref in enumerate(load_refs):
        rows = slice(place * USED, (place + 1) * USED)
        grad = ref[:, :inner].astype(F32)
        in_rows_ref[rows, :inner] = (grad * gate_factor[rows]).astype(BF16)
        in_rows_ref[rows, inner:] = (grad * up_factor[rows]).astype(BF16)
        s_share_ref[rows, :] = ref[:, inner : inner + share]


def third_rows(
    share, middle_ref, onward_ref, index_ref, w_in_ref, x_share_ref, hidden_ref, gate_factor_ref, up_factor_ref, held
):
    inner = hidden_ref.shape[1]
    held[...] = middle_ref[:, inner + share :] + onward_ref[...]
    x_share_ref[...] = held[:, pl.ds(pl.multiple_of(index_ref[0] * share, LANES), share)]
    hidden, gate_factor, up_factor = activations(dot_nn(held[...], w_in_ref[...]), hidden_ref.shape[1])
    hidden_ref[...] = hidden
    gate_factor_ref[...] = gate_factor
    up_factor_ref[...] = up_factor


def grads(middle_ref, onward_ref, *refs):
    first, third = refs[:4], refs[4:8]
    in_hbm, down_hbm, x_share, s_share, hidden, in_rows, in_ref, down_ref, sems = refs[8:]
    inner, most, share = hidden.shape[1], 3 * USED, x_share.shape[1]
    for whole, part in zip((x_share, s_share, hidden, in_rows), first):
        whole[:most, :] = part[...]
    third_x_ref, third_hidden_ref, gate_factor_ref, up_factor_ref = third
    x_share[most:, :] = third_x_ref[...]
    hidden[most:, :] = third_hidden_ref[...]
    s_share[most:, :] = middle_ref[:, inner : inner + share] + onward_ref[:, inner + share :]
    grad = (middle_ref[:, :inner] + onward_ref[:, :inner]).astype(F32)
    copies = []
    for place, factor_ref in enumerate((gate_factor_ref, up_factor_ref)):
        half = pl.ds(place * inner, inner)
        in_rows[most:, half] = (grad * factor_ref[...]).astype(BF16)
        in_ref[:, half] = dot_tn(x_share[...], in_rows[:, half]).astype(BF16)
        copies.append(pltpu.make_async_copy(in_ref.at[:, half], in_hbm.at[:, half], sems.at[place]))
        copies[-1].start()
    down_ref[...] = dot_tn(hidden[...], s_share[...]).astype(BF16)
    copies.append(pltpu.make_async_copy(down_ref, down_hbm, sems.at[2]))
    copies[-1].start()
    for copy in copies:
        copy.wait()


def to_experts(block, peers):
    slots, width = block.shape
    moved = lax.all_to_all(
        block.reshape(peers, slots // peers, width), "expert", split_axis=0, concat_axis=0, tiled=True
    )
    return moved.reshape(slots, width)


def on_device(
    replicas, tokens, out_cotangent, chosen_rows, counts, gate_weights, in_weights, down_weights
):
    tokens, cot, w_in, w_down = tokens[0], out_cotangent[0], in_weights[0], down_weights[0]
    rows, count, gates = chosen_rows[0, 0], counts[0], gate_weights[0, 0]
    peers, most = rows.shape
    slots = peers * most
    n_tokens, width = tokens.shape
    inner = w_down.shape[0]
    share = width // replicas
    on_line = replicas == 4 and share % LANES == 0
    index = lax.axis_index("dp").astype(jnp.int32).reshape(1)
    shape = jax.ShapeDtypeStruct
    vmem = pl.BlockSpec(memory_space=pltpu.VMEM)
    smem = pl.BlockSpec(memory_space=pltpu.SMEM)
    hbm = pl.BlockSpec(memory_space=pltpu.HBM)

    w_in_far = pltpu.with_memory_space_constraint(w_in, pltpu.HBM)
    picked = (rows, count, tokens, cot)
    (sent,) = call(
        pick_rows,
        [shape((slots, 2 * width), BF16)],
        [pltpu.with_memory_space_constraint(a, pltpu.HBM) for a in picked] + [gates],
        4 * slots * n_tokens * width,
        [hbm] * 4 + [vmem],
        [pltpu.VMEM(a.shape, a.dtype) for a in picked] + [pltpu.SemaphoreType.DMA((4,))],
        8,
    )
    arrived = to_experts(sent, peers)
    x_rows, pack = call(
        pack_rows,
        [shape((USED, width), BF16), shape((USED, slots), BF16)],
        (arrived,),
        2 * USED * slots * width,
        vmem=6,
    )
    short = inner + share
    hidden_grad, *loads = call(
        functools.partial(own_hidden_grad, share),
        [shape((USED, inner), F32)]
        + [
            shape((USED, short), BF16),
            shape((USED, short), BF16),
            shape((USED, short), BF16),
            shape((USED, short + share), BF16),
        ]
        * on_line,
        (index, arrived, pack, x_rows, w_down),
        2 * USED * width * (slots + inner),
        [smem] + [vmem] * 4,
        [
            pltpu.VMEM((USED, width), BF16),
        ],
        8,
    )
    if on_line:
        own, middle_load, near_load, far_load = loads
        x_far = lax.ppermute(x_rows, "dp", FAR)
        x_near = lax.ppermute(x_rows, "dp", NEAR)
        near = lax.ppermute(near_load, "dp", NEAR)
    parts = 4
    sent_back, *loads = call(
        own_rows,
        [shape((slots, width + LANES), BF16)] + [pltpu.HBM((USED, short + width), BF16)] * 2 * on_line,
        (x_rows, hidden_grad, pack, w_in_far, *loads[:2]),
        2 * USED * inner * width * 4,
        [vmem] * 3 + [hbm] + [vmem] * 2 * on_line,
        [pltpu.VMEM(w_in.shape, BF16), pltpu.SemaphoreType.DMA((parts,)), pltpu.SemaphoreType.DMA((4,))],
        16,
        [vmem] + [hbm] * 2 * on_line,
    )
    if on_line:
        own, middle_load = loads
    if on_line:
        far = lax.ppermute(far_load, "dp", FAR)
        x_near, x_far, sent_back = lax.optimization_barrier((x_near, x_far, sent_back))
    back = to_experts(sent_back, peers)
    if on_line:
        middle_load, near, sent_back = lax.optimization_barrier((middle_load, near, sent_back))
        middle = lax.ppermute(middle_load, "dp", MIDDLE)
        x_onward = lax.ppermute(x_far, "dp", ONWARD)
        onward = lax.ppermute(far, "dp", ONWARD)
    token_grad, gate_grad = call(
        combine_tokens,
        [shape((n_tokens, width), BF16), shape((peers, most), BF16)],
        (rows, count, gates, back),
        2 * slots * n_tokens * width,
        vmem=8,
    )
    if on_line:
        everyone, first = replicas * USED, 3 * USED

        w_in_held, *first_parts = call(
            functools.partial(near_rows, share),
            [
                shape(w_in.shape, BF16),
                shape((first, share), BF16),
                shape((first, share), BF16),
                shape((first, inner), BF16),
                shape((first, 2 * inner), BF16),
            ],
            (x_near, x_far, own, near, far, index, w_in_far),
            4 * first * inner * width,
            [vmem] * 5 + [smem, hbm],
            [pltpu.VMEM((first, width), BF16), pltpu.SemaphoreType.DMA((parts,))],
            16,
        )
        third_parts = call(
            functools.partial(third_rows, share),
            [
                shape((USED, share), BF16),
                shape((USED, inner), BF16),
                shape((USED, inner), F32),
                shape((USED, inner), F32),
            ],
            (middle, x_onward, index, w_in_held),
            4 * USED * inner * width,
            [vmem] * 2 + [smem, vmem],
            [pltpu.VMEM((USED, width), BF16)],
            16,
        )
        middle, token_grad = lax.optimization_barrier((middle, token_grad))
        in_grad, down_grad = call(
            grads,
            [shape((share, 2 * inner), BF16), shape((inner, share), BF16)],
            (middle, onward, *first_parts, *third_parts),
            6 * everyone * inner * share,
            None,
            [
                pltpu.VMEM((everyone, share), BF16),
                pltpu.VMEM((everyone, share), BF16),
                pltpu.VMEM((everyone, inner), BF16),
                pltpu.VMEM((everyone, 2 * inner), BF16),
                pltpu.VMEM((share, 2 * inner), BF16),
                pltpu.VMEM((inner, share), BF16),
                pltpu.SemaphoreType.DMA((3,)),
            ],
            16,
            [hbm] * 2,
        )
    else:
        x_all = lax.all_gather(x_rows, "dp", axis=0, tiled=True)
        hidden, gate_factor, up_factor = activations(dot_nn(x_all, w_in), inner)
        hidden_grad = lax.all_gather(hidden_grad, "dp", axis=0, tiled=True)
        in_rows = jnp.concatenate([hidden_grad * gate_factor, hidden_grad * up_factor], axis=1)
        x_share = lax.dynamic_slice_in_dim(x_all, index[0] * share, share, axis=1)
        scaled = dot_nn(pack, arrived[:, width : 2 * width]).astype(BF16)
        s_all = lax.all_gather(scaled, "dp", axis=0, tiled=True)
        s_share = lax.dynamic_slice_in_dim(s_all, index[0] * share, share, axis=1)
        in_grad = dot_tn(x_share, in_rows.astype(BF16)).astype(BF16)
        down_grad = dot_tn(hidden, s_share).astype(BF16)
    return (token_grad[None], gate_grad[None, None], in_grad[None], down_grad[None])


def solution(mesh):
    return jax.shard_map(
        functools.partial(on_device, mesh.shape["dp"]),
        mesh=mesh,
        in_specs=(
            P("dp", "expert", None),
            P("dp", "expert", None),
            P("dp", "expert", None, None),
            P("dp", "expert", None),
            P("dp", "expert", None, None),
            P("expert", None, None),
            P("expert", None, None),
        ),
        out_specs=(
            P("dp", "expert", None),
            P("dp", "expert", None, None),
            P("expert", "dp", None),
            P("expert", None, "dp"),
        ),
        check_vma=False,
    )
```
